128 devices in a mesh: dp: 32 (over z, y, core), mp: 4 (over x).
Axes of the slice: x: 4, y: 4, z: 4, core: 2. Of those that a mesh axis runs over, the one named last changes fastest.
Arguments:
- grads: bfloat16 [32, 32, 256, 2048], P('dp', None, None, 'mp'), may hold values from -5 to 5
- owner: int32 [32], replicated, may hold values from 0 to 31, as said below
- stats_old: float32 [96, 256, 256], P('dp', 'mp'), may hold values from -0.05 to 1.2, as said below
- prev_roots: bfloat16 [32, 256, 256], replicated, may hold values from -0.03 to 1.06, as said below
Outputs:
- stats_new: float32 [96, 256, 256], P('dp', 'mp')
- roots: bfloat16 [32, 256, 256], P(None, 'mp')
The draws below stay inside these ranges and needn't reach their ends.
Inputs may be any that keep to these rules, and one draw needn't show every extreme that they name: No owner is named by more than 3 factors, and one owner by exactly 3. `stats_old`: Symmetric. `prev_roots`: Symmetric.
All inputs are finite; a program needn't handle non-finite values.
Results may differ from the reference program's by a relative error of at most 0.00075.
Values may be sent and summed in bfloat16 or wider, within the bound.
No kernel may reach another device: no remote copies, remote signals or barrier semaphores. Data moves between devices by JAX's collectives and lax.ppermute only.
A program may use at most 128 MiB of HBM per device.

```python
import math
import jax
import jax.numpy as jnp
from jax import lax

K = 256
CB = 2048
ITERS = 2
CAP = 3
NFAC = 32
N_DP = 32


def draw_grads(key, part):
    key = jax.random.fold_in(key, 11)
    key_rows, key_vals = jax.random.split(key, 2)
    row_scale = jnp.exp(jax.random.uniform(key_rows, (NFAC, K, 1), jnp.float32, math.log(0.5), math.log(1.2)))
    values = jax.random.truncated_normal(key_vals, -4.0, 4.0, (N_DP, NFAC, K, CB), jnp.float32)
    return (values * row_scale[None]).astype(jnp.bfloat16)


def draw_owner(key, part):
    key = jax.random.fold_in(key, 37)
    key_heavy, key_slots, key_order = jax.random.split(key, 3)
    heavy = jax.random.randint(key_heavy, (), 0, N_DP)
    slot_total = (N_DP - 1) * CAP
    last_first = (N_DP - 2) * CAP
    rest = jax.random.permutation(key_slots, slot_total - 2).astype(jnp.int32) + 1
    rest = rest + (rest >= last_first).astype(jnp.int32)
    forced = jnp.array([0, last_first], dtype=jnp.int32)
    picked = jnp.concatenate([forced, rest])[:NFAC - CAP]
    others = picked // CAP
    others = others + (others >= heavy).astype(others.dtype)
    owners = jnp.concatenate([jnp.full((CAP,), heavy, dtype=jnp.int32), others.astype(jnp.int32)])
    shuffle = jax.random.permutation(key_order, NFAC)
    return owners[shuffle].astype(jnp.int32)


def symmetric_matrices(key_diag, key_noise, count, diag_lo, diag_hi, spread):
    identity = jnp.eye(K, dtype=jnp.float32)
    diag_vals = jnp.exp(jax.random.uniform(key_diag, (count, K), jnp.float32, math.log(diag_lo), math.log(diag_hi)))
    noise = spread * jax.random.truncated_normal(key_noise, -3.0, 3.0, (count, K, K), jnp.float32)
    mirrored = 0.5 * (noise + jnp.swapaxes(noise, 1, 2)) * (1.0 - identity)
    return mirrored + diag_vals[:, :, None] * identity


def draw_stats_old(key, part):
    key = jax.random.fold_in(key, 23)
    key_diag, key_noise = jax.random.split(key)
    return symmetric_matrices(key_diag, key_noise, N_DP * CAP, 0.5, 1.2, 0.015)


def draw_prev_roots(key, part):
    key = jax.random.fold_in(key, 51)
    key_diag, key_noise = jax.random.split(key)
    return symmetric_matrices(key_diag, key_noise, NFAC, 0.75, 1.05, 0.008).astype(jnp.bfloat16)


def setup_inputs(seed: int = 0) -> dict:
    splits = jax.random.split(jax.random.key(seed), 5)
    grads = draw_grads(jax.random.fold_in(splits[4], 71), 0)
    owner = draw_owner(jax.random.fold_in(splits[4], 71), 0)
    stats_old = draw_stats_old(jax.random.fold_in(splits[4], 71), 0)
    prev_roots = draw_prev_roots(jax.random.fold_in(splits[4], 71), 0)
    return dict(grads=grads, owner=owner, stats_old=stats_old, prev_roots=prev_roots)


def slot_tables(owner, slot_count, owner_count):
    factor_count = owner.shape[0]
    factor_ids = jnp.arange(factor_count, dtype=jnp.int32)
    earlier_same = (owner[:, None] == owner[None, :]) & (factor_ids[None, :] < factor_ids[:, None])
    rank_in = jnp.sum(earlier_same.astype(jnp.int32), axis=1).astype(jnp.int32)
    slot_of = (owner * slot_count + rank_in).astype(jnp.int32)
    slot_ids = jnp.arange(owner_count * slot_count, dtype=jnp.int32)
    matches = slot_of[None, :] == slot_ids[:, None]
    occupied = jnp.any(matches, axis=1)
    slot_factor = jnp.sum(jnp.where(matches, factor_ids[None, :], 0), axis=1).astype(jnp.int32)
    return slot_of, slot_factor, occupied


def product(left, right):
    return jnp.einsum("bij,bjk->bik", left, right, precision=lax.Precision.HIGHEST)


def newton_full(factor_stats, warm_start):
    identity = jnp.eye(factor_stats.shape[-1], dtype=jnp.float32)
    square = product(warm_start, warm_start)
    coupled = product(product(square, square), factor_stats)
    root = warm_start
    for iteration in range(ITERS):
        update = (5.0 * identity - coupled) * 0.25
        root = product(root, update)
        update_square = product(update, update)
        coupled = product(product(update_square, update_square), coupled)
    return root


def reference(grads, owner, stats_old, prev_roots):
    slot_of, slot_factor, occupied = slot_tables(owner, CAP, N_DP)

    def one_gram(index):
        block = jnp.take(grads, index, axis=1).astype(jnp.float32)
        return jnp.einsum("dic,djc->ij", block, block, precision=lax.Precision.HIGHEST)

    grams = lax.map(one_gram, jnp.arange(NFAC, dtype=jnp.int32))
    sums = grams * (1.0 / (N_DP * CB))
    factor_stats = jnp.take(stats_old, slot_of, axis=0) + sums
    stats_new = jnp.where(occupied[:, None, None], jnp.take(factor_stats, slot_factor, axis=0), 0.0)
    roots = newton_full(factor_stats, prev_roots.astype(jnp.float32)).astype(jnp.bfloat16)
    return (stats_new, roots)
```

```python
import jax
import jax.numpy as jnp
from jax import lax
from jax.experimental import pallas as pl
from jax.experimental.pallas import tpu as pltpu
from jax.sharding import Mesh, PartitionSpec as P

ITERS = 2
K = 256
Q = 64
L = 128
STEP = 4
CHUNK = 8
ROWS = STEP * Q + 16
CROWS = (CHUNK // STEP) * ROWS
PIECE = Q + 8
f32 = jnp.float32
bf16 = jnp.bfloat16
HI = lax.Precision.HIGHEST


def iotas(rows):
    row = lax.broadcasted_iota(jnp.int32, (rows, L), 0)
    lane = lax.broadcasted_iota(jnp.int32, (rows, L), 1)
    return row, lane


def pick_masks(m):
    row, lane = iotas(Q)
    odd = lax.rem(m, 2)
    below = (lane - Q * odd) < row
    right = lane >= Q
    from_diag = jnp.where(odd == 0, (right | below).astype(jnp.int32), (right & below).astype(jnp.int32)) > 0
    return from_diag, lane == row + Q * odd


def pack(rows, m, masks):
    t0, t1 = rows[:, :L], rows[:, L:]
    low = m < 2
    diag_tile = jnp.where(low, t0, t1)
    other = jnp.where(low, t1, t0)
    from_diag, on_diag = masks
    packed = jnp.where(from_diag, diag_tile, other)
    diag = jnp.sum(jnp.where(on_diag, diag_tile, 0.0), axis=0, keepdims=True)
    return packed, diag


def own_half(m):
    _, lane = iotas(16)
    odd = lax.rem(m, 2)
    return (lane >= Q * odd) & (lane < Q * odd + Q)


def split_diag(d):
    hi = d.astype(bf16).astype(f32)
    return (hi + pltpu.roll(d - hi, Q, 1)).astype(bf16)


def gram_rows(g_ref, k, x):
    left = jnp.concatenate([g_ref[0, k, pl.ds(pl.multiple_of(Q * lax.rem(x + s, 4), Q), Q), :] for s in range(4)], axis=0)
    return lax.dot_general(left, g_ref[0, k], (((1,), (1,)), ((), ())), preferred_element_type=f32)


def place(acc, k, d):
    row, _ = iotas(16)
    return acc + jnp.where(row == k, d, 0.0)


def gram_send_kernel(meta, g_ref, out_ref):
    x = meta[0]
    blocks = [lax.rem(x + s, 4) for s in range(4)]
    masks = [pick_masks(m) for m in blocks]
    diags = [jnp.zeros((16, L), f32) for _ in range(4)]
    for k in range(STEP):
        gram = gram_rows(g_ref, k, x)
        for s in range(4):
            packed, d = pack(gram[Q * s:Q * (s + 1)], blocks[s], masks[s])
            out_ref[s, Q * k:Q * (k + 1), :] = packed.astype(bf16)
            diags[s] = place(diags[s], k, d)
    for s in range(4):
        out_ref[s, STEP * Q:, :] = split_diag(diags[s])


def gram_keep_kernel(meta, g_ref, got_ref, own_ref, *send_refs):
    x = meta[0]
    blocks = [lax.rem(x + s, 4) for s in range(4)]
    masks = [pick_masks(m) for m in blocks]
    diags = [jnp.zeros((16, L), f32) for _ in range(4)]
    for k in range(STEP):
        gram = gram_rows(g_ref, k, x)
        rows = slice(Q * k, Q * (k + 1))
        for s in range(4):
            packed, d = pack(gram[Q * s:Q * (s + 1)], blocks[s], masks[s])
            packed = packed + got_ref[s, rows, :].astype(f32)
            if s == 0:
                own_ref[rows, :] = packed
            else:
                send_refs[s - 1][rows, :] = packed.astype(bf16)
            diags[s] = place(diags[s], k, d)
    for s in range(4):
        got = got_ref[s, STEP * Q:, :].astype(f32)
        d = diags[s] + jnp.where(own_half(blocks[s]), got + pltpu.roll(got, Q, 1), 0.0)
        if s == 0:
            own_ref[STEP * Q:, :] = d
        else:
            send_refs[s - 1][STEP * Q:, :] = split_diag(d)


def gram_params():
    return pltpu.CompilerParams(vmem_limit_bytes=48 * 2**20)


GRAM_COST = pl.CostEstimate(flops=2 * CHUNK * K * K * 512, bytes_accessed=CHUNK * K * 512 * 2 + 2**19, transcendentals=0)


def gram_send(meta, grads):
    return pl.pallas_call(
        gram_send_kernel,
        grid_spec=pltpu.PrefetchScalarGridSpec(
            num_scalar_prefetch=1,
            grid=(CHUNK // STEP,),
            in_specs=[pl.BlockSpec((1, STEP, K, 512), lambda i, meta: (0, meta[1] + i, 0, 0))],
            out_specs=pl.BlockSpec((4, ROWS, L), lambda i, meta: (0, i, 0)),
        ),
        out_shape=jax.ShapeDtypeStruct((4, CROWS, L), bf16),
        compiler_params=gram_params(),
        cost_estimate=GRAM_COST,
        name="gram_send",
    )(meta, grads)


def gram_keep(meta, grads, got):
    piece = pl.BlockSpec((ROWS, L), lambda i, meta: (i, 0))
    return pl.pallas_call(
        gram_keep_kernel,
        grid_spec=pltpu.PrefetchScalarGridSpec(
            num_scalar_prefetch=1,
            grid=(CHUNK // STEP,),
            in_specs=[
                pl.BlockSpec((1, STEP, K, 512), lambda i, meta: (0, meta[1] + i, 0, 0)),
                pl.BlockSpec((4, ROWS, L), lambda i, meta: (0, i, 0)),
            ],
            out_specs=[piece] * 4,
        ),
        out_shape=[jax.ShapeDtypeStruct((CROWS, L), f32)] + [jax.ShapeDtypeStruct((CROWS, L), bf16)] * 3,
        compiler_params=gram_params(),
        cost_estimate=GRAM_COST,
        name="gram_keep",
    )(meta, grads, got)


def rank_of(owner_ref, f, o):
    return lax.fori_loop(0, f, lambda g, n: n + (owner_ref[g] == o).astype(jnp.int32), jnp.int32(0))


def combine_kernel(scale, meta, owner_ref, *refs):
    out_ref = refs[-1]
    mine, theirs = refs[-3], refs[-2]
    x, c, zy = meta[0], meta[1], meta[2]
    masks = pick_masks(x)
    row, _ = iotas(8)
    for j in range(2 * CHUNK):
        chunk, at = divmod(j, CHUNK)
        base = (at // STEP) * ROWS
        k = at % STEP
        parts = refs[4 * chunk:4 * chunk + 4]
        main = parts[0][base + Q * k:base + Q * (k + 1), :]
        tail = parts[0][base + STEP * Q:base + ROWS, :]
        for part in parts[1:]:
            main = main + part[base + Q * k:base + Q * (k + 1), :].astype(f32)
            tail = tail + part[base + STEP * Q:base + ROWS, :].astype(f32)
        out_ref[j, :Q, :] = main * scale
        tail = tail * scale
        out_ref[j, Q:, :] = jnp.where(row == 0, tail[k:k + 1, :], 0.0)
    def fold(j, carry):
        f = c * 16 + j
        o = owner_ref[f]

        @pl.when(o // 2 == zy)
        def _():
            r = rank_of(owner_ref, f, o)
            pick = jnp.where(o % 2 == c, 1.0, 0.0)
            old = mine[r] * pick + theirs[r] * (1.0 - pick)
            packed, d = pack(old, x, masks)
            out_ref[j, :Q, :] += packed
            out_ref[j, Q:, :] += jnp.where(row == 0, d, 0.0)

        return carry

    lax.fori_loop(0, 2 * CHUNK, fold, 0)


def combine(scale, meta, owner, chunks, mine, theirs):
    args = [a for chunk in chunks for a in chunk] + [mine, theirs]
    return pl.pallas_call(
        lambda *r: combine_kernel(scale, *r),
        in_specs=[pl.BlockSpec(memory_space=pltpu.SMEM)] * 2 + [pl.BlockSpec(memory_space=pltpu.VMEM)] * len(args),
        out_specs=pl.BlockSpec(memory_space=pltpu.VMEM),
        out_shape=jax.ShapeDtypeStruct((16, PIECE, L), f32),
        name="combine",
    )(meta, owner, *args)


def unpack_kernel(meta, *refs):
    pieces, (full_ref, rows_ref, held, half) = refs[:4], refs[4:]
    x = meta[0]
    for s in range(4):
        held[lax.rem(x - s + 4, 4)] = pieces[s][...]
    row, lane = iotas(Q)
    for m in range(4):
        odd = m % 2
        part = held[m, :Q, :]
        below = (lane - Q * odd) < row
        equal = lane == row + Q * odd
        right = lane >= Q
        from_diag = (right | below) if odd == 0 else (right & below)
        diag_tile = jnp.where(from_diag, part, 0.0)
        other = jnp.where(from_diag, 0.0, part)
        if m >= 2:
            other = jnp.where(equal, 0.0, other)
        d = held[m, Q:, :]
        d = (d + pltpu.roll(d, Q, 1))[:1]
        diag_tile = diag_tile + jnp.where(equal, 0.5 * d, 0.0)
        tiles = (diag_tile, other) if m < 2 else (other, diag_tile)
        half[Q * m:Q * (m + 1), :L] = tiles[0]
        half[Q * m:Q * (m + 1), L:] = tiles[1]
    h = half[...]
    full_ref[...] = h + h.T
    rows_ref[...] = full_ref[pl.ds(pl.multiple_of(Q * x, Q), Q), :]


def unpack(meta, pieces):
    vmem = pl.BlockSpec(memory_space=pltpu.VMEM)
    return pl.pallas_call(
        unpack_kernel,
        in_specs=[pl.BlockSpec(memory_space=pltpu.SMEM)] + [vmem] * 4,
        out_specs=[vmem] * 2,
        out_shape=[jax.ShapeDtypeStruct((K, K), f32), jax.ShapeDtypeStruct((Q, K), f32)],
        scratch_shapes=[pltpu.VMEM((4, PIECE, L), f32), pltpu.VMEM((K, K), f32)],
        name="unpack",
    )(meta, *pieces)


def mm(a, b):
    return jnp.dot(a, b, precision=HI, preferred_element_type=f32)


def fourth_kernel(meta, root_ref, out_ref):
    r = root_ref[0]
    square = jnp.dot(r, r, preferred_element_type=f32)
    out_ref[...] = mm(square, square)


def fourth(meta, prev_roots):
    return pl.pallas_call(
        fourth_kernel,
        grid_spec=pltpu.PrefetchScalarGridSpec(
            num_scalar_prefetch=1,
            grid=(1,),
            in_specs=[pl.BlockSpec((1, K, K), lambda i, meta: (meta[3], 0, 0))],
            out_specs=pl.BlockSpec((K, K), lambda i, meta: (0, 0)),
        ),
        out_shape=jax.ShapeDtypeStruct((K, K), f32),
        cost_estimate=pl.CostEstimate(flops=14 * K**3, bytes_accessed=6 * K * K, transcendentals=0),
        name="fourth",
    )(meta, prev_roots)


def newton_kernel(meta, root_ref, fourth_ref, factor_ref, out_ref):
    row = lax.broadcasted_iota(jnp.int32, (K, K), 0)
    col = lax.broadcasted_iota(jnp.int32, (K, K), 1)
    five = jnp.where(row == col, 5.0, 0.0)
    coupled = mm(fourth_ref[...], factor_ref[...])
    root = root_ref[0, pl.ds(pl.multiple_of(Q * meta[0], Q), Q), :].astype(f32)
    for iteration in range(ITERS):
        update = (five - coupled) * 0.25
        root = mm(root, update)
        if iteration + 1 < ITERS:
            square = mm(update, update)
            coupled = mm(mm(square, square), coupled)
    root = root.astype(bf16)
    for j in range(16):
        out_ref[j] = root


def newton(meta, prev_roots, power, factor):
    whole = pl.BlockSpec((K, K), lambda i, meta: (0, 0))
    return pl.pallas_call(
        newton_kernel,
        grid_spec=pltpu.PrefetchScalarGridSpec(
            num_scalar_prefetch=1,
            grid=(1,),
            in_specs=[pl.BlockSpec((1, K, K), lambda i, meta: (meta[3], 0, 0)), whole, whole],
            out_specs=pl.BlockSpec((16, Q, K), lambda i, meta: (0, 0, 0)),
        ),
        out_shape=jax.ShapeDtypeStruct((16, Q, K), bf16),
        cost_estimate=pl.CostEstimate(flops=60 * K**3, bytes_accessed=2**20, transcendentals=0),
        name="newton",
    )(meta, prev_roots, power, factor)


def slots_kernel(meta, owner_ref, rows_ref, own_ref, other_ref):
    c, zy = meta[1], meta[2]
    own_ref[...] = jnp.zeros(own_ref.shape, f32)
    other_ref[...] = jnp.zeros(other_ref.shape, f32)
    for target, ref in ((2 * zy + c, own_ref), (2 * zy + 1 - c, other_ref)):
        def step(f, n, target=target, ref=ref):
            hit = owner_ref[f] == target

            @pl.when(hit & (f // 16 == c))
            def _():
                ref[n] = rows_ref[lax.rem(f, 16)]

            return n + hit.astype(jnp.int32)

        lax.fori_loop(0, 32, step, jnp.int32(0))


def slots(meta, owner, rows):
    vmem = pl.BlockSpec(memory_space=pltpu.VMEM)
    shape = jax.ShapeDtypeStruct((3, Q, K), f32)
    return pl.pallas_call(
        slots_kernel,
        in_specs=[pl.BlockSpec(memory_space=pltpu.SMEM)] * 2 + [vmem],
        out_specs=[vmem] * 2,
        out_shape=[shape, shape],
        name="slots",
    )(meta, owner, rows)


def swap(a):
    return lax.ppermute(a, "c", [(0, 1), (1, 0)])


def turn(a, s):
    return lax.ppermute(a, "x", [(i, (i + s) % 4) for i in range(4)])


def body(grads, owner, stats_old, prev_roots):
    z, y, c, x = (lax.axis_index(a) for a in ("z", "y", "c", "x"))
    zy = z * 4 + y
    scale = 1.0 / (32 * 2048)
    meta = jnp.stack([x, c, zy, c * 16 + zy]).astype(jnp.int32)

    def gram_meta(core, chunk):
        return jnp.stack([x, (core * 16 + chunk * CHUNK) // STEP]).astype(jnp.int32)

    their_old = swap(stats_old)
    sends = [gram_send(gram_meta(1 - c, h), grads) for h in range(2)]
    gots = [swap(a) for a in sends]
    kept = [gram_keep(gram_meta(c, h), grads, gots[h]) for h in range(2)]
    chunks = [[part[0]] + [turn(part[s], s) for s in (1, 2, 3)] for part in kept]
    outgoing = combine(scale, meta, owner, chunks, stats_old, their_old)
    arrived = lax.all_to_all(outgoing, ("z", "y"), 0, 0, tiled=True)
    piece = jnp.sum(arrived, axis=0)
    power = fourth(meta, prev_roots)
    pieces = [piece] + [turn(piece, s) for s in (1, 2, 3)]
    factor, rows = unpack(meta, pieces)
    all_rows = lax.all_gather(rows, ("z", "y"), axis=0, tiled=False)
    root = newton(meta, prev_roots, power, factor)
    mine = lax.all_to_all(root, ("z", "y"), 0, 0, tiled=True)
    theirs = swap(mine)
    roots = jnp.concatenate([jnp.where(c == 0, mine, theirs), jnp.where(c == 0, theirs, mine)], axis=0)
    own, other = slots(meta, owner, all_rows)
    stats_new = own + swap(other)
    return stats_new, roots


def solution(mesh):
    fine = Mesh(mesh.devices.reshape(4, 4, 2, 4), ("z", "y", "c", "x"))
    dp = ("z", "y", "c")
    return jax.shard_map(
        body,
        mesh=fine,
        in_specs=(P(dp, None, None, "x"), P(), P(dp, "x", None), P()),
        out_specs=(P(dp, "x", None), P(None, "x", None)),
        check_vma=False,
    )
```

```python
import jax
import jax.numpy as jnp
from jax import lax
from jax.experimental import pallas as pl
from jax.experimental.pallas import tpu as pltpu
from jax.sharding import Mesh, PartitionSpec as P

ITERS = 2
K = 256
Q = 64
L = 128
STEP = 4
CHUNK = 8
ROWS = STEP * Q + 16
CROWS = (CHUNK // STEP) * ROWS
PIECE = Q + 8
f32 = jnp.float32
bf16 = jnp.bfloat16
HI = lax.Precision.HIGHEST


def iotas(rows):
    row = lax.broadcasted_iota(jnp.int32, (rows, L), 0)
    lane = lax.broadcasted_iota(jnp.int32, (rows, L), 1)
    return row, lane


def pick_masks(m):
    row, lane = iotas(Q)
    odd = lax.rem(m, 2)
    below = (lane - Q * odd) < row
    right = lane >= Q
    from_diag = jnp.where(odd == 0, (right | below).astype(jnp.int32), (right & below).astype(jnp.int32)) > 0
    return from_diag, lane == row + Q * odd


def pack(rows, m, masks):
    t0, t1 = rows[:, :L], rows[:, L:]
    low = m < 2
    diag_tile = jnp.where(low, t0, t1)
    other = jnp.where(low, t1, t0)
    from_diag, on_diag = masks
    packed = jnp.where(from_diag, diag_tile, other)
    diag = jnp.sum(jnp.where(on_diag, diag_tile, 0.0), axis=0, keepdims=True)
    return packed, diag


def own_half(m):
    _, lane = iotas(16)
    odd = lax.rem(m, 2)
    return (lane >= Q * odd) & (lane < Q * odd + Q)


def split_diag(d):
    hi = d.astype(bf16).astype(f32)
    return (hi + pltpu.roll(d - hi, Q, 1)).astype(bf16)


def gram_rows(g_ref, k, x):
    left = jnp.concatenate([g_ref[0, k, pl.ds(pl.multiple_of(Q * lax.rem(x + s, 4), Q), Q), :] for s in range(4)], axis=0)
    return lax.dot_general(left, g_ref[0, k], (((1,), (1,)), ((), ())), preferred_element_type=f32)


def place(acc, k, d):
    row, _ = iotas(16)
    return acc + jnp.where(row == k, d, 0.0)


def gram_send_kernel(meta, g_ref, out_ref):
    x = meta[0]
    blocks = [lax.rem(x + s, 4) for s in range(4)]
    masks = [pick_masks(m) for m in blocks]
    diags = [jnp.zeros((16, L), f32) for _ in range(4)]
    for k in range(STEP):
        gram = gram_rows(g_ref, k, x)
        for s in range(4):
            packed, d = pack(gram[Q * s:Q * (s + 1)], blocks[s], masks[s])
            out_ref[s, Q * k:Q * (k + 1), :] = packed.astype(bf16)
            diags[s] = place(diags[s], k, d)
    for s in range(4):
        out_ref[s, STEP * Q:, :] = split_diag(diags[s])


def gram_keep_kernel(meta, g_ref, got_ref, own_ref, *send_refs):
    x = meta[0]
    blocks = [lax.rem(x + s, 4) for s in range(4)]
    masks = [pick_masks(m) for m in blocks]
    diags = [jnp.zeros((16, L), f32) for _ in range(4)]
    for k in range(STEP):
        gram = gram_rows(g_ref, k, x)
        rows = slice(Q * k, Q * (k + 1))
        for s in range(4):
            packed, d = pack(gram[Q * s:Q * (s + 1)], blocks[s], masks[s])
            packed = packed + got_ref[s, rows, :].astype(f32)
            if s == 0:
                own_ref[rows, :] = packed
            else:
                send_refs[s - 1][rows, :] = packed.astype(bf16)
            diags[s] = place(diags[s], k, d)
    for s in range(4):
        got = got_ref[s, STEP * Q:, :].astype(f32)
        d = diags[s] + jnp.where(own_half(blocks[s]), got + pltpu.roll(got, Q, 1), 0.0)
        if s == 0:
            own_ref[STEP * Q:, :] = d
        else:
            send_refs[s - 1][STEP * Q:, :] = split_diag(d)


def gram_params():
    return pltpu.CompilerParams(vmem_limit_bytes=48 * 2**20)


GRAM_COST = pl.CostEstimate(flops=2 * CHUNK * K * K * 512, bytes_accessed=CHUNK * K * 512 * 2 + 2**19, transcendentals=0)


def gram_send(meta, grads):
    return pl.pallas_call(
        gram_send_kernel,
        grid_spec=pltpu.PrefetchScalarGridSpec(
            num_scalar_prefetch=1,
            grid=(CHUNK // STEP,),
            in_specs=[pl.BlockSpec((1, STEP, K, 512), lambda i, meta: (0, meta[1] + i, 0, 0))],
            out_specs=pl.BlockSpec((4, ROWS, L), lambda i, meta: (0, i, 0)),
        ),
        out_shape=jax.ShapeDtypeStruct((4, CROWS, L), bf16),
        compiler_params=gram_params(),
        cost_estimate=GRAM_COST,
        name="gram_send",
    )(meta, grads)


def gram_keep(meta, grads, got):
    piece = pl.BlockSpec((ROWS, L), lambda i, meta: (i, 0))
    return pl.pallas_call(
        gram_keep_kernel,
        grid_spec=pltpu.PrefetchScalarGridSpec(
            num_scalar_prefetch=1,
            grid=(CHUNK // STEP,),
            in_specs=[
                pl.BlockSpec((1, STEP, K, 512), lambda i, meta: (0, meta[1] + i, 0, 0)),
                pl.BlockSpec((4, ROWS, L), lambda i, meta: (0, i, 0)),
            ],
            out_specs=[piece] * 4,
        ),
        out_shape=[jax.ShapeDtypeStruct((CROWS, L), f32)] + [jax.ShapeDtypeStruct((CROWS, L), bf16)] * 3,
        compiler_params=gram_params(),
        cost_estimate=GRAM_COST,
        name="gram_keep",
    )(meta, grads, got)


def rank_of(owner_ref, f, o):
    return lax.fori_loop(0, f, lambda g, n: n + (owner_ref[g] == o).astype(jnp.int32), jnp.int32(0))


def combine_kernel(scale, meta, owner_ref, *refs):
    out_ref = refs[-1]
    mine, theirs = refs[-3], refs[-2]
    x, c, zy = meta[0], meta[1], meta[2]
    masks = pick_masks(x)
    row, _ = iotas(8)
    for j in range(2 * CHUNK):
        chunk, at = divmod(j, CHUNK)
        base = (at // STEP) * ROWS
        k = at % STEP
        parts = refs[4 * chunk:4 * chunk + 4]
        main = parts[0][base + Q * k:base + Q * (k + 1), :]
        tail = parts[0][base + STEP * Q:base + ROWS, :]
        for part in parts[1:]:
            main = main + part[base + Q * k:base + Q * (k + 1), :].astype(f32)
            tail = tail + part[base + STEP * Q:base + ROWS, :].astype(f32)
        out_ref[j, :Q, :] = main * scale
        tail = tail * scale
        out_ref[j, Q:, :] = jnp.where(row == 0, tail[k:k + 1, :], 0.0)
    def fold(j, carry):
        f = c * 16 + j
        o = owner_ref[f]

        @pl.when(o // 2 == zy)
        def _():
            r = rank_of(owner_ref, f, o)
            pick = jnp.where(o % 2 == c, 1.0, 0.0)
            old = mine[r] * pick + theirs[r] * (1.0 - pick)
            packed, d = pack(old, x, masks)
            out_ref[j, :Q, :] += packed
            out_ref[j, Q:, :] += jnp.where(row == 0, d, 0.0)

        return carry

    lax.fori_loop(0, 2 * CHUNK, fold, 0)


def combine(scale, meta, owner, chunks, mine, theirs):
    args = [a for chunk in chunks for a in chunk] + [mine, theirs]
    return pl.pallas_call(
        lambda *r: combine_kernel(scale, *r),
        in_specs=[pl.BlockSpec(memory_space=pltpu.SMEM)] * 2 + [pl.BlockSpec(memory_space=pltpu.VMEM)] * len(args),
        out_specs=pl.BlockSpec(memory_space=pltpu.VMEM),
        out_shape=jax.ShapeDtypeStruct((16, PIECE, L), f32),
        name="combine",
    )(meta, owner, *args)


def unpack(x, pieces, held, half):
    for s in range(4):
        held[lax.rem(x - s + 4, 4)] = pieces[s][...]
    row, lane = iotas(Q)
    for m in range(4):
        odd = m % 2
        part = held[m, :Q, :]
        below = (lane - Q * odd) < row
        equal = lane == row + Q * odd
        right = lane >= Q
        from_diag = (right | below) if odd == 0 else (right & below)
        diag_tile = jnp.where(from_diag, part, 0.0)
        other = jnp.where(from_diag, 0.0, part)
        if m >= 2:
            other = jnp.where(equal, 0.0, other)
        d = held[m, Q:, :]
        d = (d + pltpu.roll(d, Q, 1))[:1]
        diag_tile = diag_tile + jnp.where(equal, 0.5 * d, 0.0)
        tiles = (diag_tile, other) if m < 2 else (other, diag_tile)
        half[Q * m:Q * (m + 1), :L] = tiles[0]
        half[Q * m:Q * (m + 1), L:] = tiles[1]
    h = half[...]
    return h + h.T


def mm(a, b):
    return jnp.dot(a, b, precision=HI, preferred_element_type=f32)


def fourth_kernel(meta, root_ref, out_ref):
    r = root_ref[0]
    square = jnp.dot(r, r, preferred_element_type=f32)
    out_ref[...] = mm(square, square)


def fourth(meta, prev_roots):
    return pl.pallas_call(
        fourth_kernel,
        grid_spec=pltpu.PrefetchScalarGridSpec(
            num_scalar_prefetch=1,
            grid=(1,),
            in_specs=[pl.BlockSpec((1, K, K), lambda i, meta: (meta[3], 0, 0))],
            out_specs=pl.BlockSpec((K, K), lambda i, meta: (0, 0)),
        ),
        out_shape=jax.ShapeDtypeStruct((K, K), f32),
        cost_estimate=pl.CostEstimate(flops=14 * K**3, bytes_accessed=6 * K * K, transcendentals=0),
        name="fourth",
    )(meta, prev_roots)


def newton_kernel(meta, root_ref, fourth_ref, *refs):
    pieces, (out_ref, held, full) = refs[:4], refs[4:]
    x = meta[0]
    mine = pl.ds(pl.multiple_of(Q * x, Q), Q)
    factor = unpack(x, pieces, held, full)
    full[...] = factor
    rows = full[mine, :]
    high = rows.astype(bf16)
    low = (rows - high.astype(f32)).astype(bf16)
    row = lax.broadcasted_iota(jnp.int32, (K, K), 0)
    col = lax.broadcasted_iota(jnp.int32, (K, K), 1)
    five = jnp.where(row == col, 5.0, 0.0)
    coupled = mm(fourth_ref[...], factor)
    root = root_ref[0, mine, :].astype(f32)
    for iteration in range(ITERS):
        update = (five - coupled) * 0.25
        root = mm(root, update)
        if iteration + 1 < ITERS:
            square = mm(update, update)
            coupled = mm(mm(square, square), coupled)
    root = root.astype(bf16)
    for j in range(16):
        out_ref[j, :Q] = root
        out_ref[j, Q:2 * Q] = high
        out_ref[j, 2 * Q:] = low


def newton(meta, prev_roots, power, pieces):
    whole = pl.BlockSpec((K, K), lambda i, meta: (0, 0))
    piece = pl.BlockSpec((PIECE, L), lambda i, meta: (0, 0))
    return pl.pallas_call(
        newton_kernel,
        grid_spec=pltpu.PrefetchScalarGridSpec(
            num_scalar_prefetch=1,
            grid=(1,),
            in_specs=[pl.BlockSpec((1, K, K), lambda i, meta: (meta[3], 0, 0)), whole] + [piece] * 4,
            out_specs=pl.BlockSpec((16, 3 * Q, K), lambda i, meta: (0, 0, 0)),
            scratch_shapes=[pltpu.VMEM((4, PIECE, L), f32), pltpu.VMEM((K, K), f32)],
        ),
        out_shape=jax.ShapeDtypeStruct((16, 3 * Q, K), bf16),
        compiler_params=gram_params(),
        cost_estimate=pl.CostEstimate(flops=60 * K**3, bytes_accessed=2**21, transcendentals=0),
        name="newton",
    )(meta, prev_roots, power, *pieces)


def finish_kernel(meta, owner_ref, mine, theirs, stats_ref, roots_ref, held, root_sems, slot_sems):
    c, zy = meta[1], meta[2]
    target = 2 * zy + c

    def root_copy(src, core, sem):
        return pltpu.make_async_copy(src.at[:, pl.ds(0, Q), :], roots_ref.at[pl.ds(16 * core, 16)], root_sems.at[sem])

    root_copy(mine, c, 0).start()
    root_copy(theirs, 1 - c, 1).start()

    def slot_copy(src, f, n):
        return pltpu.make_async_copy(src.at[lax.rem(f, 16), pl.ds(Q, 2 * Q), :], held.at[n], slot_sems.at[n])

    def step(f, n):
        hit = owner_ref[f] == target

        @pl.when(hit & (f // 16 == c))
        def _():
            slot_copy(mine, f, n).start()

        @pl.when(hit & (f // 16 != c))
        def _():
            slot_copy(theirs, f, n).start()

        return n + hit.astype(jnp.int32)

    count = lax.fori_loop(0, 32, step, jnp.int32(0))
    for n in range(3):
        @pl.when(n < count)
        def _():
            slot_copy(mine, 0, n).wait()
            stats_ref[n] = held[n, :Q].astype(f32) + held[n, Q:].astype(f32)

        @pl.when(n >= count)
        def _():
            stats_ref[n] = jnp.zeros((Q, K), f32)

    root_copy(mine, c, 0).wait()
    root_copy(theirs, 1 - c, 1).wait()


def finish(meta, owner, mine, theirs):
    smem = pl.BlockSpec(memory_space=pltpu.SMEM)
    any_space = pl.BlockSpec(memory_space=pl.ANY)
    return pl.pallas_call(
        finish_kernel,
        in_specs=[smem, smem, any_space, any_space],
        out_specs=[pl.BlockSpec(memory_space=pltpu.VMEM), any_space],
        out_shape=[jax.ShapeDtypeStruct((3, Q, K), f32), jax.ShapeDtypeStruct((32, Q, K), bf16)],
        scratch_shapes=[
            pltpu.VMEM((3, 2 * Q, K), bf16),
            pltpu.SemaphoreType.DMA((2,)),
            pltpu.SemaphoreType.DMA((3,)),
        ],
        name="finish",
    )(meta, owner, mine, theirs)


def swap(a):
    return lax.ppermute(a, "c", [(0, 1), (1, 0)])


def turn(a, s):
    return lax.ppermute(a, "x", [(i, (i + s) % 4) for i in range(4)])


def body(grads, owner, stats_old, prev_roots):
    z, y, c, x = (lax.axis_index(a) for a in ("z", "y", "c", "x"))
    zy = z * 4 + y
    scale = 1.0 / (32 * 2048)
    meta = jnp.stack([x, c, zy, c * 16 + zy]).astype(jnp.int32)

    def gram_meta(core, chunk):
        return jnp.stack([x, (core * 16 + chunk * CHUNK) // STEP]).astype(jnp.int32)

    their_old = swap(stats_old)
    sends = [gram_send(gram_meta(1 - c, h), grads) for h in range(2)]
    gots = [swap(a) for a in sends]
    kept = [gram_keep(gram_meta(c, h), grads, gots[h]) for h in range(2)]
    chunks = [[part[0]] + [turn(part[s], s) for s in (1, 2, 3)] for part in kept]
    outgoing = combine(scale, meta, owner, chunks, stats_old, their_old)
    arrived = lax.all_to_all(outgoing, ("z", "y"), 0, 0, tiled=True)
    piece = jnp.sum(arrived, axis=0)
    power = fourth(meta, prev_roots)
    pieces = [piece] + [turn(piece, s) for s in (1, 2, 3)]
    held = newton(meta, prev_roots, power, pieces)
    mine = lax.all_to_all(held, ("z", "y"), 0, 0, tiled=True)
    return finish(meta, owner, mine, swap(mine))


def solution(mesh):
    fine = Mesh(mesh.devices.reshape(4, 4, 2, 4), ("z", "y", "c", "x"))
    dp = ("z", "y", "c")
    return jax.shard_map(
        body,
        mesh=fine,
        in_specs=(P(dp, None, None, "x"), P(), P(dp, "x", None), P()),
        out_specs=(P(dp, "x", None), P(None, "x", None)),
        check_vma=False,
    )
```

```python
import jax
import jax.numpy as jnp
from jax import lax
from jax.experimental import pallas as pl
from jax.experimental.pallas import tpu as pltpu
from jax.sharding import Mesh, PartitionSpec as P

ITERS = 2
K = 256
Q = 64
L = 128
STEP = 4
CHUNK = 8
SWAP = K + 16
SEND = SWAP + Q
PIECE = K + 8
f32 = jnp.float32
bf16 = jnp.bfloat16
HI = lax.Precision.HIGHEST


def iotas(rows):
    row = lax.broadcasted_iota(jnp.int32, (rows, L), 0)
    lane = lax.broadcasted_iota(jnp.int32, (rows, L), 1)
    return row, lane


def pick_masks(m):
    row, lane = iotas(Q)
    odd = m % 2
    below = ((lane - Q * odd) < row).astype(jnp.int32)
    right = (lane >= Q).astype(jnp.int32)
    from_diag = jnp.maximum(right, below) * (1 - odd) + right * below * odd
    return from_diag > 0, lane == row + Q * odd


def pack(rows, m, masks):
    t0, t1 = rows[:, :L], rows[:, L:]
    if isinstance(m, int):
        diag_tile, other = (t0, t1) if m < 2 else (t1, t0)
    else:
        diag_tile = jnp.where(m < 2, t0, t1)
        other = jnp.where(m < 2, t1, t0)
    from_diag, on_diag = masks
    packed = jnp.where(from_diag, diag_tile, other)
    diag = jnp.sum(jnp.where(on_diag, diag_tile, 0.0), axis=0, keepdims=True)
    return packed, diag


def split_diag(d):
    hi = d.astype(bf16).astype(f32)
    return (hi + pltpu.roll(d - hi, Q, 1)).astype(bf16)


def place(acc, k, d):
    row, _ = iotas(16)
    return acc + jnp.where(row == k, d, 0.0)


def gram_of(g_ref, k):
    g = g_ref[0, k]
    return lax.dot_general(g, g, (((1,), (1,)), ((), ())), preferred_element_type=f32)


def gram_send_kernel(meta, g_ref, out_ref):
    masks = [pick_masks(m) for m in range(4)]
    for k in range(STEP):
        gram = gram_of(g_ref, k)
        diag = jnp.zeros((16, L), f32)
        for m in range(4):
            packed, d = pack(gram[Q * m:Q * (m + 1)], m, masks[m])
            out_ref[k, Q * m:Q * (m + 1), :] = packed.astype(bf16)
            diag = place(diag, m, d)
        out_ref[k, K:, :] = split_diag(diag)


def rank_of(owner_ref, f, o):
    return lax.fori_loop(0, f, lambda g, n: n + (owner_ref[g] == o).astype(jnp.int32), jnp.int32(0))


def gram_keep_kernel(scale, base, meta, owner_ref, g_ref, got_ref, mine, theirs, *refs):
    out_ref, parts, diags = refs[-3:]
    x, c, zy = meta[0], meta[1], meta[2]
    masks = [pick_masks(m) for m in range(4)]
    row, lane = iotas(16)
    own_half = (lane >= Q * (row % 2)) & (lane < Q * (row % 2) + Q)
    quarter = pl.ds(pl.multiple_of(Q * x, Q), Q)
    for k in range(STEP):
        gram = gram_of(g_ref, k)
        diag = jnp.zeros((16, L), f32)
        for m in range(4):
            rows = slice(Q * m, Q * (m + 1))
            packed, d = pack(gram[rows], m, masks[m])
            packed = (packed + got_ref[k, rows, :].astype(f32)) * scale
            parts[k, m] = packed
            out_ref[k, rows, :] = packed.astype(bf16)
            diag = place(diag, m, d)
        got = got_ref[k, K:, :].astype(f32)
        diags[k] = (diag + jnp.where(own_half, got + pltpu.roll(got, Q, 1), 0.0)) * scale
    for k in range(STEP):
        f = c * 16 + base + pl.program_id(0) * STEP + k
        o = owner_ref[f]

        @pl.when(o // 2 == zy)
        def _(k=k, f=f, o=o):
            r = rank_of(owner_ref, f, o)
            pick = jnp.where(o % 2 == c, 1.0, 0.0)
            old = mine[r] * pick + theirs[r] * (1.0 - pick)
            packed, d = pack(old, x, pick_masks(x))
            parts[k, x] += packed
            diags[k] += jnp.where(row == x, d, 0.0)

    for k in range(STEP):
        part = parts[k, x]
        high = part.astype(bf16)
        out_ref[k, quarter, :] = high
        out_ref[k, SWAP:, :] = (part - high.astype(f32)).astype(bf16)
        out_ref[k, K:SWAP, :] = split_diag(diags[k])


def params(mib):
    return pltpu.CompilerParams(vmem_limit_bytes=mib * 2**20)


GRAM_COST = pl.CostEstimate(flops=2 * CHUNK * K * K * 512, bytes_accessed=CHUNK * K * 512 * 2 + 2**19, transcendentals=0)


def gram_send(meta, grads):
    return pl.pallas_call(
        gram_send_kernel,
        grid_spec=pltpu.PrefetchScalarGridSpec(
            num_scalar_prefetch=1,
            grid=(CHUNK // STEP,),
            in_specs=[pl.BlockSpec((1, STEP, K, 512), lambda i, meta: (0, meta[0] + i, 0, 0))],
            out_specs=pl.BlockSpec((STEP, SWAP, L), lambda i, meta: (i, 0, 0)),
        ),
        out_shape=jax.ShapeDtypeStruct((CHUNK, SWAP, L), bf16),
        compiler_params=params(48),
        cost_estimate=GRAM_COST,
        name="gram_send",
    )(meta, grads)


def gram_keep(scale, chunk, meta, owner, grads, got, mine, theirs, before=None):
    per = CHUNK // STEP
    old = pl.BlockSpec((3, Q, K), lambda i, meta, owner: (0, 0, 0))
    in_specs = [
        pl.BlockSpec((1, STEP, K, 512), lambda i, meta, owner: (0, meta[1] * (16 // STEP) + chunk * per + i, 0, 0)),
        pl.BlockSpec((STEP, SWAP, L), lambda i, meta, owner: (i, 0, 0)),
        old,
        old,
    ]
    args = [grads, got, mine, theirs]
    aliases = {}
    if before is not None:
        in_specs.append(pl.BlockSpec(memory_space=pl.ANY))
        args.append(before)
        aliases = {6: 0}

    def kernel(*refs):
        gram_keep_kernel(scale, chunk * CHUNK, *refs)

    return pl.pallas_call(
        kernel,
        grid_spec=pltpu.PrefetchScalarGridSpec(
            num_scalar_prefetch=2,
            grid=(per,),
            in_specs=in_specs,
            out_specs=pl.BlockSpec((STEP, SEND, L), lambda i, meta, owner: (chunk * per + i, 0, 0)),
            scratch_shapes=[pltpu.VMEM((STEP, 4, Q, L), f32), pltpu.VMEM((STEP, 16, L), f32)],
        ),
        out_shape=jax.ShapeDtypeStruct((16, SEND, L), bf16),
        input_output_aliases=aliases,
        compiler_params=params(48),
        cost_estimate=GRAM_COST,
        name="gram_keep",
    )(meta, owner, *args)


def plane_sum_kernel(arrived, out_ref):
    for m in range(4):
        rows = slice(Q * m, Q * (m + 1))
        total = arrived[0, rows, :].astype(f32)
        for j in range(1, 16):
            total = total + arrived[j, rows, :].astype(f32)
        for y in range(4):
            total = total + arrived[4 * y + m, SWAP:, :].astype(f32)
        out_ref[rows, :] = total
    total = arrived[0, K:SWAP, :].astype(f32)
    for j in range(1, 16):
        total = total + arrived[j, K:SWAP, :].astype(f32)
    out_ref[K:, :] = total[:8]


def plane_sum(arrived):
    return pl.pallas_call(
        plane_sum_kernel,
        grid=(1,),
        in_specs=[pl.BlockSpec((16, SEND, L), lambda i: (0, 0, 0))],
        out_specs=pl.BlockSpec((PIECE, L), lambda i: (0, 0)),
        out_shape=jax.ShapeDtypeStruct((PIECE, L), f32),
        compiler_params=params(16),
        name="plane_sum",
    )(arrived)


def unpack(total, half):
    row, lane = iotas(Q)
    ends = total[K:]
    ends = ends + pltpu.roll(ends, Q, 1)
    for m in range(4):
        odd = m % 2
        part = total[Q * m:Q * (m + 1)]
        below = (lane - Q * odd) < row
        equal = lane == row + Q * odd
        right = lane >= Q
        from_diag = (right | below) if odd == 0 else (right & below)
        diag_tile = jnp.where(from_diag, part, 0.0)
        other = jnp.where(from_diag, 0.0, part)
        if m >= 2:
            other = jnp.where(equal, 0.0, other)
        diag_tile = diag_tile + jnp.where(equal, 0.5 * ends[m:m + 1], 0.0)
        tiles = (diag_tile, other) if m < 2 else (other, diag_tile)
        half[Q * m:Q * (m + 1), :L] = tiles[0]
        half[Q * m:Q * (m + 1), L:] = tiles[1]
    h = half[...]
    return h + h.T


def mm(a, b):
    return jnp.dot(a, b, precision=HI, preferred_element_type=f32)


def fourth_kernel(meta, root_ref, out_ref, copy_ref):
    r = root_ref[0]
    copy_ref[...] = r
    square = jnp.dot(r, r, preferred_element_type=f32)
    out_ref[...] = mm(square, square)


def fourth(meta, prev_roots):
    whole = pl.BlockSpec((K, K), lambda i, meta: (0, 0))
    return pl.pallas_call(
        fourth_kernel,
        grid_spec=pltpu.PrefetchScalarGridSpec(
            num_scalar_prefetch=1,
            grid=(1,),
            in_specs=[pl.BlockSpec((1, K, K), lambda i, meta: (meta[3], 0, 0))],
            out_specs=[whole, whole],
        ),
        out_shape=[jax.ShapeDtypeStruct((K, K), f32), jax.ShapeDtypeStruct((K, K), bf16)],
        compiler_params=params(8),
        cost_estimate=pl.CostEstimate(flops=14 * K**3, bytes_accessed=6 * K * K, transcendentals=0),
        name="fourth",
    )(meta, prev_roots)


def newton_kernel(meta, root_ref, fourth_ref, *refs):
    pieces, (out_ref, held, half) = refs[:4], refs[4:]
    z = meta[4]
    for s in range(4):
        held[lax.rem(z - s + 4, 4)] = pieces[s][...]
    factor = unpack(((held[0] + held[1]) + held[2]) + held[3], half)
    high = factor.astype(bf16)
    low = (factor - high.astype(f32)).astype(bf16)
    row = lax.broadcasted_iota(jnp.int32, (K, K), 0)
    col = lax.broadcasted_iota(jnp.int32, (K, K), 1)
    five = jnp.where(row == col, 5.0, 0.0)
    coupled = mm(fourth_ref[...], factor)
    root = root_ref[...].astype(f32)
    for iteration in range(ITERS):
        update = (five - coupled) * 0.25
        root = mm(root, update)
        if iteration + 1 < ITERS:
            square = mm(update, update)
            coupled = mm(mm(square, square), coupled)
    root = root.astype(bf16)
    for j in range(16):
        rows = slice(Q * (j % 4), Q * (j % 4 + 1))
        out_ref[j, :Q] = root[rows]
        out_ref[j, Q:2 * Q] = high[rows]
        out_ref[j, 2 * Q:] = low[rows]


def newton(meta, root, power, pieces):
    whole = pl.BlockSpec((K, K), lambda i, meta: (0, 0))
    piece = pl.BlockSpec((PIECE, L), lambda i, meta: (0, 0))
    return pl.pallas_call(
        newton_kernel,
        grid_spec=pltpu.PrefetchScalarGridSpec(
            num_scalar_prefetch=1,
            grid=(1,),
            in_specs=[whole, whole] + [piece] * 4,
            out_specs=pl.BlockSpec((16, 3 * Q, K), lambda i, meta: (0, 0, 0)),
            scratch_shapes=[pltpu.VMEM((4, PIECE, L), f32), pltpu.VMEM((K, K), f32)],
        ),
        out_shape=jax.ShapeDtypeStruct((16, 3 * Q, K), bf16),
        compiler_params=params(16),
        cost_estimate=pl.CostEstimate(flops=60 * K**3, bytes_accessed=2**21, transcendentals=0),
        name="newton",
    )(meta, root, power, *pieces)


ANY = pl.BlockSpec(memory_space=pl.ANY)
SMEM = pl.BlockSpec(memory_space=pltpu.SMEM)
ROOTS = jax.ShapeDtypeStruct((32, Q, K), bf16)


def root_copy(src, roots_ref, core, sem):
    return pltpu.make_async_copy(src.at[:, pl.ds(0, Q), :], roots_ref.at[pl.ds(16 * core, 16)], sem)


def own_roots_kernel(meta, mine, roots_ref, sem):
    copy = root_copy(mine, roots_ref, meta[1], sem)
    copy.start()
    copy.wait()


def own_roots(meta, mine):
    return pl.pallas_call(
        own_roots_kernel,
        in_specs=[SMEM, ANY],
        out_specs=ANY,
        out_shape=ROOTS,
        scratch_shapes=[pltpu.SemaphoreType.DMA],
        compiler_params=params(4),
        cost_estimate=pl.CostEstimate(flops=0, bytes_accessed=2**20, transcendentals=0),
        name="own_roots",
    )(meta, mine)


def finish_kernel(meta, owner_ref, mine, theirs, before, stats_ref, roots_ref, held, root_sem, slot_sems):
    c, zy = meta[1], meta[2]
    target = 2 * zy + c
    copy = root_copy(theirs, roots_ref, 1 - c, root_sem)
    copy.start()

    def slot_copy(src, f, n):
        return pltpu.make_async_copy(src.at[lax.rem(f, 16), pl.ds(Q, 2 * Q), :], held.at[n], slot_sems.at[n])

    def step(f, n):
        hit = owner_ref[f] == target

        @pl.when(hit & (f // 16 == c))
        def _():
            slot_copy(mine, f, n).start()

        @pl.when(hit & (f // 16 != c))
        def _():
            slot_copy(theirs, f, n).start()

        return n + hit.astype(jnp.int32)

    count = lax.fori_loop(0, 32, step, jnp.int32(0))
    for n in range(3):
        @pl.when(n < count)
        def _():
            slot_copy(mine, 0, n).wait()
            stats_ref[n] = held[n, :Q].astype(f32) + held[n, Q:].astype(f32)

        @pl.when(n >= count)
        def _():
            stats_ref[n] = jnp.zeros((Q, K), f32)

    copy.wait()


def finish(meta, owner, mine, theirs, roots):
    return pl.pallas_call(
        finish_kernel,
        in_specs=[SMEM, SMEM, ANY, ANY, ANY],
        out_specs=[pl.BlockSpec(memory_space=pltpu.VMEM), ANY],
        out_shape=[jax.ShapeDtypeStruct((3, Q, K), f32), ROOTS],
        scratch_shapes=[
            pltpu.VMEM((3, 2 * Q, K), bf16),
            pltpu.SemaphoreType.DMA,
            pltpu.SemaphoreType.DMA((3,)),
        ],
        input_output_aliases={4: 1},
        compiler_params=params(4),
        name="finish",
    )(meta, owner, mine, theirs, roots)


def swap(a):
    return lax.ppermute(a, "c", [(0, 1), (1, 0)])


def turn(a, s):
    return lax.ppermute(a, "z", [(i, (i + s) % 4) for i in range(4)])


def body(grads, owner, stats_old, prev_roots):
    z, y, c, x = (lax.axis_index(a) for a in ("z", "y", "c", "x"))
    scale = 1.0 / (32 * 2048)
    meta = jnp.stack([x, c, z * 4 + y, c * 16 + y * 4 + x, z]).astype(jnp.int32)
    per_core = 16 // STEP

    def send_meta(chunk):
        return jnp.stack([(1 - c) * per_core + chunk * (CHUNK // STEP)]).astype(jnp.int32)

    their_old = swap(stats_old)
    gots = [swap(gram_send(send_meta(h), grads)) for h in range(2)]
    outgoing = None
    for h in range(2):
        outgoing = gram_keep(scale, h, meta, owner, grads, gots[h], stats_old, their_old, outgoing)
    arrived = lax.all_to_all(outgoing, ("y", "x"), 0, 0, tiled=True)
    piece = plane_sum(arrived)
    power, root = fourth(meta, prev_roots)
    pieces = [piece] + [turn(piece, s) for s in (1, 2, 3)]
    mine = lax.all_to_all(newton(meta, root, power, pieces), ("y", "x"), 0, 0, tiled=True)
    return finish(meta, owner, mine, swap(mine), own_roots(meta, mine))


def solution(mesh):
    fine = Mesh(mesh.devices.reshape(4, 4, 2, 4), ("z", "y", "c", "x"))
    dp = ("z", "y", "c")
    return jax.shard_map(
        body,
        mesh=fine,
        in_specs=(P(dp, None, None, "x"), P(), P(dp, "x", None), P()),
        out_specs=(P(dp, "x", None), P(None, "x", None)),
        check_vma=False,
    )
```

```python
import jax
import jax.numpy as jnp
from jax import lax
from jax.experimental import pallas as pl
from jax.experimental.pallas import tpu as pltpu
from jax.sharding import Mesh, PartitionSpec as P

ITERS = 2
K = 256
Q = 64
L = 128
STEP = 4
SWAP = K + 16
SEND = SWAP + Q
PIECE = K + 8
f32 = jnp.float32
bf16 = jnp.bfloat16
HI = lax.Precision.HIGHEST


def iotas(rows):
    row = lax.broadcasted_iota(jnp.int32, (rows, L), 0)
    lane = lax.broadcasted_iota(jnp.int32, (rows, L), 1)
    return row, lane


def pick_masks(m):
    row, lane = iotas(Q)
    odd = m % 2
    below = ((lane - Q * odd) < row).astype(jnp.int32)
    right = (lane >= Q).astype(jnp.int32)
    from_diag = jnp.maximum(right, below) * (1 - odd) + right * below * odd
    return from_diag > 0, lane == row + Q * odd


def pack(rows, m, masks):
    t0, t1 = rows[:, :L], rows[:, L:]
    if isinstance(m, int):
        diag_tile, other = (t0, t1) if m < 2 else (t1, t0)
    else:
        diag_tile = jnp.where(m < 2, t0, t1)
        other = jnp.where(m < 2, t1, t0)
    from_diag, on_diag = masks
    packed = jnp.where(from_diag, diag_tile, other)
    diag = jnp.sum(jnp.where(on_diag, diag_tile, 0.0), axis=0, keepdims=True)
    return packed, diag


def split_diag(d):
    hi = d.astype(bf16).astype(f32)
    return (hi + pltpu.roll(d - hi, Q, 1)).astype(bf16)


def place(acc, k, d):
    row, _ = iotas(16)
    return acc + jnp.where(row == k, d, 0.0)


def gram_of(g_ref, k):
    g = g_ref[0, k]
    return lax.dot_general(g, g, (((1,), (1,)), ((), ())), preferred_element_type=f32)


def gram_pack(gram, out_ref, k, masks, dtype):
    diag = jnp.zeros((16, L), f32)
    for m in range(4):
        packed, d = pack(gram[Q * m:Q * (m + 1)], m, masks[m])
        out_ref[k, Q * m:Q * (m + 1), :] = packed.astype(dtype)
        diag = place(diag, m, d)
    return diag


def gram_send_kernel(meta, g_ref, out_ref):
    masks = [pick_masks(m) for m in range(4)]
    for k in range(STEP):
        out_ref[k, K:, :] = split_diag(gram_pack(gram_of(g_ref, k), out_ref, k, masks, bf16))


def rank_of(owner_ref, f, o):
    return lax.fori_loop(0, f, lambda g, n: n + (owner_ref[g] == o).astype(jnp.int32), jnp.int32(0))


def gram_keep_kernel(meta, g_ref, out_ref):
    masks = [pick_masks(m) for m in range(4)]
    for k in range(STEP):
        out_ref[k, K:, :] = gram_pack(gram_of(g_ref, k), out_ref, k, masks, f32)


def merge_kernel(scale, meta, owner_ref, own_ref, got_ref, mine, theirs, out_ref, parts, diags):
    x, c, zy = meta[0], meta[1], meta[2]
    quarter = pl.ds(pl.multiple_of(Q * x, Q), Q)
    row, lane = iotas(16)
    own_half = (lane >= Q * (row % 2)) & (lane < Q * (row % 2) + Q)
    for j in range(16):
        out_ref[j, :K, :] = ((own_ref[j, :K, :] + got_ref[j, :K, :].astype(f32)) * scale).astype(bf16)
        got = got_ref[j, K:, :].astype(f32)
        got = jnp.where(own_half, got + pltpu.roll(got, Q, 1), 0.0)
        diags[j] = (own_ref[j, K:, :] + got) * scale
        parts[j] = (own_ref[j, quarter, :] + got_ref[j, quarter, :].astype(f32)) * scale

    def fold(j, carry):
        f = c * 16 + j
        o = owner_ref[f]

        @pl.when(o // 2 == zy)
        def _():
            r = rank_of(owner_ref, f, o)
            pick = jnp.where(o % 2 == c, 1.0, 0.0)
            old = mine[r] * pick + theirs[r] * (1.0 - pick)
            packed, d = pack(old, x, pick_masks(x))
            parts[j] += packed
            diags[j] += jnp.where(row == x, d, 0.0)

        return carry

    lax.fori_loop(0, 16, fold, 0)
    for j in range(16):
        high = parts[j].astype(bf16)
        out_ref[j, quarter, :] = high
        out_ref[j, SWAP:, :] = (parts[j] - high.astype(f32)).astype(bf16)
        out_ref[j, K:SWAP, :] = split_diag(diags[j])


def params(mib):
    return pltpu.CompilerParams(vmem_limit_bytes=mib * 2**20)


GRAM_COST = pl.CostEstimate(flops=32 * K * K * 512, bytes_accessed=16 * K * 512 * 2 + 2**21, transcendentals=0)


def gram_send(meta, grads):
    per = 16 // STEP
    return pl.pallas_call(
        gram_send_kernel,
        grid_spec=pltpu.PrefetchScalarGridSpec(
            num_scalar_prefetch=1,
            grid=(per,),
            in_specs=[pl.BlockSpec((1, STEP, K, 512), lambda i, meta: (0, (1 - meta[1]) * per + i, 0, 0))],
            out_specs=pl.BlockSpec((STEP, SWAP, L), lambda i, meta: (i, 0, 0)),
        ),
        out_shape=jax.ShapeDtypeStruct((16, SWAP, L), bf16),
        compiler_params=params(48),
        cost_estimate=GRAM_COST,
        name="gram_send",
    )(meta, grads)


def gram_keep(meta, grads):
    per = 16 // STEP
    return pl.pallas_call(
        gram_keep_kernel,
        grid_spec=pltpu.PrefetchScalarGridSpec(
            num_scalar_prefetch=1,
            grid=(per,),
            in_specs=[pl.BlockSpec((1, STEP, K, 512), lambda i, meta: (0, meta[1] * per + i, 0, 0))],
            out_specs=pl.BlockSpec((STEP, SWAP, L), lambda i, meta: (i, 0, 0)),
        ),
        out_shape=jax.ShapeDtypeStruct((16, SWAP, L), f32),
        compiler_params=params(48),
        cost_estimate=GRAM_COST,
        name="gram_keep",
    )(meta, grads)


def merge(scale, meta, owner, own, got, mine, theirs):
    whole = pl.BlockSpec((16, SWAP, L), lambda i, *_: (0, 0, 0))
    old = pl.BlockSpec((3, Q, K), lambda i, *_: (0, 0, 0))

    def kernel(*refs):
        merge_kernel(scale, *refs)

    return pl.pallas_call(
        kernel,
        grid_spec=pltpu.PrefetchScalarGridSpec(
            num_scalar_prefetch=2,
            grid=(1,),
            in_specs=[whole, whole, old, old],
            out_specs=pl.BlockSpec((16, SEND, L), lambda i, *_: (0, 0, 0)),
            scratch_shapes=[pltpu.VMEM((16, Q, L), f32), pltpu.VMEM((16, 16, L), f32)],
        ),
        out_shape=jax.ShapeDtypeStruct((16, SEND, L), bf16),
        compiler_params=params(24),
        cost_estimate=pl.CostEstimate(flops=2**20, bytes_accessed=2**22, transcendentals=0),
        name="merge",
    )(meta, owner, own, got, mine, theirs)


def plane_sum_kernel(arrived, out_ref):
    for m in range(4):
        rows = slice(Q * m, Q * (m + 1))
        total = arrived[0, rows, :].astype(f32)
        for j in range(1, 16):
            total = total + arrived[j, rows, :].astype(f32)
        for y in range(4):
            total = total + arrived[4 * y + m, SWAP:, :].astype(f32)
        out_ref[rows, :] = total
    total = arrived[0, K:SWAP, :].astype(f32)
    for j in range(1, 16):
        total = total + arrived[j, K:SWAP, :].astype(f32)
    out_ref[K:, :] = total[:8]


def plane_sum(arrived):
    return pl.pallas_call(
        plane_sum_kernel,
        grid=(1,),
        in_specs=[pl.BlockSpec((16, SEND, L), lambda i: (0, 0, 0))],
        out_specs=pl.BlockSpec((PIECE, L), lambda i: (0, 0)),
        out_shape=jax.ShapeDtypeStruct((PIECE, L), f32),
        compiler_params=params(16),
        name="plane_sum",
    )(arrived)


def unpack(total, half):
    row, lane = iotas(Q)
    ends = total[K:]
    ends = ends + pltpu.roll(ends, Q, 1)
    for m in range(4):
        odd = m % 2
        part = total[Q * m:Q * (m + 1)]
        below = (lane - Q * odd) < row
        equal = lane == row + Q * odd
        right = lane >= Q
        from_diag = (right | below) if odd == 0 else (right & below)
        diag_tile = jnp.where(from_diag, part, 0.0)
        other = jnp.where(from_diag, 0.0, part)
        if m >= 2:
            other = jnp.where(equal, 0.0, other)
        diag_tile = diag_tile + jnp.where(equal, 0.5 * ends[m:m + 1], 0.0)
        tiles = (diag_tile, other) if m < 2 else (other, diag_tile)
        half[Q * m:Q * (m + 1), :L] = tiles[0]
        half[Q * m:Q * (m + 1), L:] = tiles[1]
    h = half[...]
    return h + h.T


def mm(a, b):
    return jnp.dot(a, b, precision=HI, preferred_element_type=f32)


def fourth_kernel(meta, root_ref, out_ref, copy_ref):
    r = root_ref[0]
    copy_ref[...] = r
    square = jnp.dot(r, r, preferred_element_type=f32)
    out_ref[...] = mm(square, square)


def fourth(meta, prev_roots):
    whole = pl.BlockSpec((K, K), lambda i, meta: (0, 0))
    return pl.pallas_call(
        fourth_kernel,
        grid_spec=pltpu.PrefetchScalarGridSpec(
            num_scalar_prefetch=1,
            grid=(1,),
            in_specs=[pl.BlockSpec((1, K, K), lambda i, meta: (meta[3], 0, 0))],
            out_specs=[whole, whole],
        ),
        out_shape=[jax.ShapeDtypeStruct((K, K), f32), jax.ShapeDtypeStruct((K, K), bf16)],
        compiler_params=params(8),
        cost_estimate=pl.CostEstimate(flops=14 * K**3, bytes_accessed=6 * K * K, transcendentals=0),
        name="fourth",
    )(meta, prev_roots)


def newton_kernel(meta, root_ref, fourth_ref, *refs):
    pieces, (out_ref, held, half) = refs[:4], refs[4:]
    z = meta[4]
    for s in range(4):
        held[lax.rem(z - s + 4, 4)] = pieces[s][...]
    factor = unpack(((held[0] + held[1]) + held[2]) + held[3], half)
    high = factor.astype(bf16)
    low = (factor - high.astype(f32)).astype(bf16)
    row = lax.broadcasted_iota(jnp.int32, (K, K), 0)
    col = lax.broadcasted_iota(jnp.int32, (K, K), 1)
    five = jnp.where(row == col, 5.0, 0.0)
    coupled = mm(fourth_ref[...], factor)
    root = root_ref[...].astype(f32)
    for iteration in range(ITERS):
        update = (five - coupled) * 0.25
        root = mm(root, update)
        if iteration + 1 < ITERS:
            square = mm(update, update)
            coupled = mm(mm(square, square), coupled)
    root = root.astype(bf16)
    for j in range(16):
        rows = slice(Q * (j % 4), Q * (j % 4 + 1))
        out_ref[j, :Q] = root[rows]
        out_ref[j, Q:2 * Q] = high[rows]
        out_ref[j, 2 * Q:] = low[rows]


def newton(meta, root, power, pieces):
    whole = pl.BlockSpec((K, K), lambda i, meta: (0, 0))
    piece = pl.BlockSpec((PIECE, L), lambda i, meta: (0, 0))
    return pl.pallas_call(
        newton_kernel,
        grid_spec=pltpu.PrefetchScalarGridSpec(
            num_scalar_prefetch=1,
            grid=(1,),
            in_specs=[whole, whole] + [piece] * 4,
            out_specs=pl.BlockSpec((16, 3 * Q, K), lambda i, meta: (0, 0, 0)),
            scratch_shapes=[pltpu.VMEM((4, PIECE, L), f32), pltpu.VMEM((K, K), f32)],
        ),
        out_shape=jax.ShapeDtypeStruct((16, 3 * Q, K), bf16),
        compiler_params=params(16),
        cost_estimate=pl.CostEstimate(flops=60 * K**3, bytes_accessed=2**21, transcendentals=0),
        name="newton",
    )(meta, root, power, *pieces)


ANY = pl.BlockSpec(memory_space=pl.ANY)
ROOTS = jax.ShapeDtypeStruct((32, Q, K), bf16)


def root_copies(src, roots_ref, core, sems):
    return [
        pltpu.make_async_copy(
            src.at[pl.ds(4 * i, 4), pl.ds(0, Q), :], roots_ref.at[pl.ds(16 * core + 4 * i, 4)], sems.at[i]
        )
        for i in range(4)
    ]


def own_roots_kernel(meta, mine, roots_ref, sems):
    copies = root_copies(mine, roots_ref, meta[1], sems)
    for copy in copies:
        copy.start()
    for copy in copies:
        copy.wait()


ARRIVED = pl.BlockSpec((16, 3 * Q, K), lambda i, *_: (0, 0, 0))


def own_roots(meta, mine):
    return pl.pallas_call(
        own_roots_kernel,
        grid_spec=pltpu.PrefetchScalarGridSpec(
            num_scalar_prefetch=1,
            grid=(1,),
            in_specs=[ARRIVED],
            out_specs=ANY,
            scratch_shapes=[pltpu.SemaphoreType.DMA((4,))],
        ),
        out_shape=ROOTS,
        compiler_params=params(16),
        cost_estimate=pl.CostEstimate(flops=0, bytes_accessed=2**20, transcendentals=0),
        name="own_roots",
    )(meta, mine)


def finish_kernel(meta, owner_ref, mine, theirs, before, stats_ref, roots_ref, held, sems, slot_sems):
    c, zy = meta[1], meta[2]
    target = 2 * zy + c
    copies = root_copies(theirs, roots_ref, 1 - c, sems)
    for copy in copies:
        copy.start()

    def rows_of(src, f):
        j = lax.rem(f, 16)
        return src[j, Q:2 * Q, :].astype(f32) + src[j, 2 * Q:, :].astype(f32)

    def step(f, n):
        hit = owner_ref[f] == target

        @pl.when(hit & (f // 16 == c))
        def _():
            held[n] = rows_of(mine, f)

        @pl.when(hit & (f // 16 != c))
        def _():
            held[n] = rows_of(theirs, f)

        return n + hit.astype(jnp.int32)

    count = lax.fori_loop(0, 32, step, jnp.int32(0))
    out = [pltpu.make_async_copy(held.at[n], stats_ref.at[n], slot_sems.at[n]) for n in range(3)]
    for n in range(3):
        @pl.when(n >= count)
        def _():
            held[n] = jnp.zeros((Q, K), f32)

        out[n].start()
    for copy in out + copies:
        copy.wait()


def finish(meta, owner, mine, theirs, roots):
    return pl.pallas_call(
        finish_kernel,
        grid_spec=pltpu.PrefetchScalarGridSpec(
            num_scalar_prefetch=2,
            grid=(1,),
            in_specs=[ARRIVED, ARRIVED, ANY],
            out_specs=[ANY, ANY],
            scratch_shapes=[
                pltpu.VMEM((3, Q, K), f32),
                pltpu.SemaphoreType.DMA((4,)),
                pltpu.SemaphoreType.DMA((3,)),
            ],
        ),
        out_shape=[jax.ShapeDtypeStruct((3, Q, K), f32), ROOTS],
        input_output_aliases={4: 1},
        compiler_params=params(16),
        name="finish",
    )(meta, owner, mine, theirs, roots)


def swap(a):
    return lax.ppermute(a, "c", [(0, 1), (1, 0)])


def turn(a, s):
    return lax.ppermute(a, "z", [(i, (i + s) % 4) for i in range(4)])


def body(grads, owner, stats_old, prev_roots):
    z, y, c, x = (lax.axis_index(a) for a in ("z", "y", "c", "x"))
    scale = 1.0 / (32 * 2048)
    meta = jnp.stack([x, c, z * 4 + y, c * 16 + y * 4 + x, z]).astype(jnp.int32)
    their_old = swap(stats_old)
    got = swap(gram_send(meta, grads))
    own = gram_keep(meta, grads)
    outgoing = merge(scale, meta, owner, own, got, stats_old, their_old)
    arrived = lax.all_to_all(outgoing, ("y", "x"), 0, 0, tiled=True)
    piece = plane_sum(arrived)
    power, root = fourth(meta, prev_roots)
    pieces = [piece] + [turn(piece, s) for s in (1, 2, 3)]
    mine = lax.all_to_all(newton(meta, root, power, pieces), ("y", "x"), 0, 0, tiled=True)
    return finish(meta, owner, mine, swap(mine), own_roots(meta, mine))


def solution(mesh):
    fine = Mesh(mesh.devices.reshape(4, 4, 2, 4), ("z", "y", "c", "x"))
    dp = ("z", "y", "c")
    return jax.shard_map(
        body,
        mesh=fine,
        in_specs=(P(dp, None, None, "x"), P(), P(dp, "x", None), P()),
        out_specs=(P(dp, "x", None), P(None, "x", None)),
        check_vma=False,
    )
```

```python
import jax
import jax.numpy as jnp
from jax import lax
from jax.experimental import pallas as pl
from jax.experimental.pallas import tpu as pltpu
from jax.sharding import Mesh, PartitionSpec as P

ITERS = 2
K = 256
Q = 64
L = 128
STEP = 8
PART = 2
SWAP = K + 32
SENT = K + 16
SEND = SENT + Q
PIECE = K + 8
f32 = jnp.float32
bf16 = jnp.bfloat16
HI = lax.Precision.HIGHEST


def iotas(rows):
    row = lax.broadcasted_iota(jnp.int32, (rows, L), 0)
    lane = lax.broadcasted_iota(jnp.int32, (rows, L), 1)
    return row, lane


def pick_masks(m):
    row, lane = iotas(Q)
    odd = m % 2
    below = ((lane - Q * odd) < row).astype(jnp.int32)
    right = (lane >= Q).astype(jnp.int32)
    from_diag = jnp.maximum(right, below) * (1 - odd) + right * below * odd
    return from_diag > 0, lane == row + Q * odd


def pack(rows, m, masks):
    t0, t1 = rows[:, :L], rows[:, L:]
    if isinstance(m, int):
        diag_tile, other = (t0, t1) if m < 2 else (t1, t0)
    else:
        diag_tile = jnp.where(m < 2, t0, t1)
        other = jnp.where(m < 2, t1, t0)
    from_diag, on_diag = masks
    packed = jnp.where(from_diag, diag_tile, other)
    spread = jnp.where(on_diag, diag_tile, 0.0)
    diag = spread[:8]
    for i in range(8, Q, 8):
        diag = diag + spread[i:i + 8]
    return packed, diag


def split_diag(d):
    hi = d.astype(bf16).astype(f32)
    return (hi + pltpu.roll(d - hi, Q, 1)).astype(bf16)


def gram_of(g_refs, k):
    g = g_refs[k // PART][0, k % PART]
    return lax.dot_general(g, g, (((1,), (1,)), ((), ())), preferred_element_type=f32)


def gram_pack(gram, out_ref, k, masks, dtype):
    diags = []
    for m in range(4):
        packed, d = pack(gram[Q * m:Q * (m + 1)], m, masks[m])
        out_ref[k, Q * m:Q * (m + 1), :] = packed.astype(dtype)
        diags.append(d)
    return jnp.concatenate(diags, axis=0)


def gram_send_kernel(meta, *refs):
    g_refs, out_ref = refs[:-1], refs[-1]
    masks = [pick_masks(m) for m in range(4)]
    for k in range(STEP):
        out_ref[k, K:, :] = split_diag(gram_pack(gram_of(g_refs, k), out_ref, k, masks, bf16))


def rank_of(owner_ref, f, o):
    return lax.fori_loop(0, f, lambda g, n: n + (owner_ref[g] == o).astype(jnp.int32), jnp.int32(0))


def gram_keep_kernel(meta, *refs):
    g_refs, out_ref = refs[:-1], refs[-1]
    masks = [pick_masks(m) for m in range(4)]
    for k in range(STEP):
        out_ref[k, K:, :] = gram_pack(gram_of(g_refs, k), out_ref, k, masks, f32)


def merge_kernel(scale, meta, owner_ref, own_ref, got_ref, mine, theirs, out_ref, parts, diags):
    x, c, zy = meta[0], meta[1], meta[2]
    quarter = pl.ds(pl.multiple_of(Q * x, Q), Q)
    owners = [owner_ref[c * 16 + j] for j in range(16)]
    row, lane = iotas(32)
    odd = (row // 8) % 2
    own_half = (lane >= Q * odd) & (lane < Q * odd + Q)
    for j in range(16):
        out_ref[j, :K, :] = ((own_ref[j, :K, :] + got_ref[j, :K, :].astype(f32)) * scale).astype(bf16)
        got = got_ref[j, K:, :].astype(f32)
        got = jnp.where(own_half, got + pltpu.roll(got, Q, 1), 0.0)
        diags[j] = (own_ref[j, K:, :] + got) * scale
        parts[j] = (own_ref[j, quarter, :] + got_ref[j, quarter, :].astype(f32)) * scale
    for j in range(16):
        @pl.when(owners[j] // 2 == zy)
        def _(j=j):
            o = owners[j]
            r = rank_of(owner_ref, c * 16 + j, o)
            pick = jnp.where(o % 2 == c, 1.0, 0.0)
            old = mine[r] * pick + theirs[r] * (1.0 - pick)
            packed, d = pack(old, x, pick_masks(x))
            parts[j] += packed
            diags[j, pl.ds(pl.multiple_of(8 * x, 8), 8), :] += d

    last, _ = iotas(16)
    for j in range(16):
        high = parts[j].astype(bf16)
        out_ref[j, quarter, :] = high
        out_ref[j, SENT:, :] = (parts[j] - high.astype(f32)).astype(bf16)
        diag = jnp.zeros((16, L), f32)
        for m in range(4):
            diag = jnp.where(last == m, jnp.sum(diags[j, 8 * m:8 * m + 8, :], axis=0, keepdims=True), diag)
        out_ref[j, K:SENT, :] = split_diag(diag)


def params(mib):
    return pltpu.CompilerParams(vmem_limit_bytes=mib * 2**20)


GRAM_COST = pl.CostEstimate(flops=32 * K * K * 512, bytes_accessed=16 * K * 512 * 2 + 2**21, transcendentals=0)


def gram_call(kernel, core_of, dtype, name, meta, grads):
    parts = STEP // PART
    per = 16 // PART

    def part(p):
        return pl.BlockSpec((1, PART, K, 512), lambda i, meta: (0, core_of(meta[1]) * per + i * parts + p, 0, 0))

    return pl.pallas_call(
        kernel,
        grid_spec=pltpu.PrefetchScalarGridSpec(
            num_scalar_prefetch=1,
            grid=(16 // STEP,),
            in_specs=[part(p) for p in range(parts)],
            out_specs=pl.BlockSpec((STEP, SWAP, L), lambda i, meta: (i, 0, 0)),
        ),
        out_shape=jax.ShapeDtypeStruct((16, SWAP, L), dtype),
        compiler_params=params(48),
        cost_estimate=GRAM_COST,
        name=name,
    )(meta, *([grads] * parts))


def merge(scale, meta, owner, own, got, mine, theirs):
    whole = pl.BlockSpec((16, SWAP, L), lambda i, *_: (0, 0, 0))
    old = pl.BlockSpec((3, Q, K), lambda i, *_: (0, 0, 0))

    def kernel(*refs):
        merge_kernel(scale, *refs)

    return pl.pallas_call(
        kernel,
        grid_spec=pltpu.PrefetchScalarGridSpec(
            num_scalar_prefetch=2,
            grid=(1,),
            in_specs=[whole, whole, old, old],
            out_specs=pl.BlockSpec((16, SEND, L), lambda i, *_: (0, 0, 0)),
            scratch_shapes=[pltpu.VMEM((16, Q, L), f32), pltpu.VMEM((16, 32, L), f32)],
        ),
        out_shape=jax.ShapeDtypeStruct((16, SEND, L), bf16),
        compiler_params=params(24),
        cost_estimate=pl.CostEstimate(flops=2**20, bytes_accessed=2**22, transcendentals=0),
        name="merge",
    )(meta, owner, own, got, mine, theirs)


def plane_sum_kernel(arrived, out_ref):
    for m in range(4):
        rows = slice(Q * m, Q * (m + 1))
        total = arrived[0, rows, :].astype(f32)
        for j in range(1, 16):
            total = total + arrived[j, rows, :].astype(f32)
        for y in range(4):
            total = total + arrived[4 * m + y, SENT:, :].astype(f32)
        out_ref[rows, :] = total
    total = arrived[0, K:SENT, :].astype(f32)
    for j in range(1, 16):
        total = total + arrived[j, K:SENT, :].astype(f32)
    out_ref[K:, :] = total[:8]


def plane_sum(arrived):
    return pl.pallas_call(
        plane_sum_kernel,
        grid=(1,),
        in_specs=[pl.BlockSpec((16, SEND, L), lambda i: (0, 0, 0))],
        out_specs=pl.BlockSpec((PIECE, L), lambda i: (0, 0)),
        out_shape=jax.ShapeDtypeStruct((PIECE, L), f32),
        compiler_params=params(16),
        name="plane_sum",
    )(arrived)


def unpack(total, half):
    row, lane = iotas(Q)
    ends = total[K:]
    ends = ends + pltpu.roll(ends, Q, 1)
    for m in range(4):
        odd = m % 2
        part = total[Q * m:Q * (m + 1)]
        below = (lane - Q * odd) < row
        equal = lane == row + Q * odd
        right = lane >= Q
        from_diag = (right | below) if odd == 0 else (right & below)
        diag_tile = jnp.where(from_diag, part, 0.0)
        other = jnp.where(from_diag, 0.0, part)
        if m >= 2:
            other = jnp.where(equal, 0.0, other)
        diag_tile = diag_tile + jnp.where(equal, 0.5 * ends[m:m + 1], 0.0)
        tiles = (diag_tile, other) if m < 2 else (other, diag_tile)
        half[Q * m:Q * (m + 1), :L] = tiles[0]
        half[Q * m:Q * (m + 1), L:] = tiles[1]
    h = half[...]
    return h + h.T


def mm(a, b):
    return jnp.dot(a, b, precision=HI, preferred_element_type=f32)


def fourth_kernel(meta, root_ref, out_ref, copy_ref):
    r = root_ref[0]
    copy_ref[...] = r
    square = jnp.dot(r, r, preferred_element_type=f32)
    out_ref[...] = mm(square, square)


def fourth(meta, prev_roots):
    whole = pl.BlockSpec((K, K), lambda i, meta: (0, 0))
    return pl.pallas_call(
        fourth_kernel,
        grid_spec=pltpu.PrefetchScalarGridSpec(
            num_scalar_prefetch=1,
            grid=(1,),
            in_specs=[pl.BlockSpec((1, K, K), lambda i, meta: (meta[3], 0, 0))],
            out_specs=[whole, whole],
        ),
        out_shape=[jax.ShapeDtypeStruct((K, K), f32), jax.ShapeDtypeStruct((K, K), bf16)],
        compiler_params=params(8),
        cost_estimate=pl.CostEstimate(flops=14 * K**3, bytes_accessed=6 * K * K, transcendentals=0),
        name="fourth",
    )(meta, prev_roots)


def newton_kernel(meta, root_ref, fourth_ref, *refs):
    pieces, (out_ref, held, half) = refs[:4], refs[4:]
    z = meta[4]
    for s in range(4):
        held[lax.rem(z - s + 4, 4)] = pieces[s][...]
    factor = unpack(((held[0] + held[1]) + held[2]) + held[3], half)
    high = factor.astype(bf16)
    low = (factor - high.astype(f32)).astype(bf16)
    row = lax.broadcasted_iota(jnp.int32, (K, K), 0)
    col = lax.broadcasted_iota(jnp.int32, (K, K), 1)
    five = jnp.where(row == col, 5.0, 0.0)
    coupled = mm(fourth_ref[...], factor)
    root = root_ref[...].astype(f32)
    for iteration in range(ITERS):
        update = (five - coupled) * 0.25
        root = mm(root, update)
        if iteration + 1 < ITERS:
            square = mm(update, update)
            coupled = mm(mm(square, square), coupled)
    root = root.astype(bf16)
    for j in range(16):
        rows = slice(Q * (j // 4), Q * (j // 4 + 1))
        out_ref[j, :Q] = root[rows]
        out_ref[j, Q:2 * Q] = high[rows]
        out_ref[j, 2 * Q:] = low[rows]


def newton(meta, root, power, pieces):
    whole = pl.BlockSpec((K, K), lambda i, meta: (0, 0))
    piece = pl.BlockSpec((PIECE, L), lambda i, meta: (0, 0))
    return pl.pallas_call(
        newton_kernel,
        grid_spec=pltpu.PrefetchScalarGridSpec(
            num_scalar_prefetch=1,
            grid=(1,),
            in_specs=[whole, whole] + [piece] * 4,
            out_specs=pl.BlockSpec((16, 3 * Q, K), lambda i, meta: (0, 0, 0)),
            scratch_shapes=[pltpu.VMEM((4, PIECE, L), f32), pltpu.VMEM((K, K), f32)],
        ),
        out_shape=jax.ShapeDtypeStruct((16, 3 * Q, K), bf16),
        compiler_params=params(16),
        cost_estimate=pl.CostEstimate(flops=60 * K**3, bytes_accessed=2**21, transcendentals=0),
        name="newton",
    )(meta, root, power, *pieces)


ANY = pl.BlockSpec(memory_space=pl.ANY)
ROOTS = jax.ShapeDtypeStruct((32, Q, K), bf16)


def root_copies(src, roots_ref, core, sems):
    return [
        pltpu.make_async_copy(
            src.at[pl.ds(4 * i, 4), pl.ds(0, Q), :], roots_ref.at[pl.ds(16 * core + 4 * i, 4)], sems.at[i]
        )
        for i in range(4)
    ]


def own_roots_kernel(meta, mine, roots_ref, sems):
    copies = root_copies(mine, roots_ref, meta[1], sems)
    for copy in copies:
        copy.start()
    for copy in copies:
        copy.wait()


ARRIVED = pl.BlockSpec((16, 3 * Q, K), lambda i, *_: (0, 0, 0))


def own_roots(meta, mine):
    return pl.pallas_call(
        own_roots_kernel,
        grid_spec=pltpu.PrefetchScalarGridSpec(
            num_scalar_prefetch=1,
            grid=(1,),
            in_specs=[ARRIVED],
            out_specs=ANY,
            scratch_shapes=[pltpu.SemaphoreType.DMA((4,))],
        ),
        out_shape=ROOTS,
        compiler_params=params(16),
        cost_estimate=pl.CostEstimate(flops=0, bytes_accessed=2**20, transcendentals=0),
        name="own_roots",
    )(meta, mine)


def finish_kernel(meta, owner_ref, mine, theirs, before, stats_ref, roots_ref, held, sems, slot_sems):
    c, zy = meta[1], meta[2]
    target = 2 * zy + c
    copies = root_copies(theirs, roots_ref, 1 - c, sems)
    for copy in copies:
        copy.start()

    def rows_of(src, f):
        j = lax.rem(f, 16)
        return src[j, Q:2 * Q, :].astype(f32) + src[j, 2 * Q:, :].astype(f32)

    count = jnp.int32(0)
    slot = [jnp.int32(0)] * 3
    for f in range(32):
        hit = owner_ref[f] == target
        slot = [jnp.where(hit & (count == n), f, slot[n]) for n in range(3)]
        count = count + hit.astype(jnp.int32)
    out = [pltpu.make_async_copy(held.at[n], stats_ref.at[n], slot_sems.at[n]) for n in range(3)]
    for n in range(3):
        near = slot[n] // 16 == c

        @pl.when((n < count) & near)
        def _(n=n):
            held[n] = rows_of(mine, slot[n])

        @pl.when((n < count) & jnp.logical_not(near))
        def _(n=n):
            held[n] = rows_of(theirs, slot[n])

        @pl.when(n >= count)
        def _(n=n):
            held[n] = jnp.zeros((Q, K), f32)

        out[n].start()
    for copy in out + copies:
        copy.wait()


def finish(meta, owner, mine, theirs, roots):
    return pl.pallas_call(
        finish_kernel,
        grid_spec=pltpu.PrefetchScalarGridSpec(
            num_scalar_prefetch=2,
            grid=(1,),
            in_specs=[ARRIVED, ARRIVED, ANY],
            out_specs=[ANY, ANY],
            scratch_shapes=[
                pltpu.VMEM((3, Q, K), f32),
                pltpu.SemaphoreType.DMA((4,)),
                pltpu.SemaphoreType.DMA((3,)),
            ],
        ),
        out_shape=[jax.ShapeDtypeStruct((3, Q, K), f32), ROOTS],
        input_output_aliases={4: 1},
        compiler_params=params(16),
        name="finish",
    )(meta, owner, mine, theirs, roots)


def swap(a):
    return lax.ppermute(a, "c", [(0, 1), (1, 0)])


def turn(a, s):
    return lax.ppermute(a, "z", [(i, (i + s) % 4) for i in range(4)])


def body(grads, owner, stats_old, prev_roots):
    z, y, c, x = (lax.axis_index(a) for a in ("z", "y", "c", "x"))
    scale = 1.0 / (32 * 2048)
    meta = jnp.stack([x, c, z * 4 + y, c * 16 + x * 4 + y, z]).astype(jnp.int32)
    their_old = swap(stats_old)
    got = swap(gram_call(gram_send_kernel, lambda core: 1 - core, bf16, "gram_send", meta, grads))
    own = gram_call(gram_keep_kernel, lambda core: core, f32, "gram_keep", meta, grads)
    outgoing = merge(scale, meta, owner, own, got, stats_old, their_old)
    arrived = lax.all_to_all(outgoing, ("x", "y"), 0, 0, tiled=True)
    piece = plane_sum(arrived)
    power, root = fourth(meta, prev_roots)
    pieces = [piece] + [turn(piece, s) for s in (1, 2, 3)]
    mine = lax.all_to_all(newton(meta, root, power, pieces), ("x", "y"), 0, 0, tiled=True)
    return finish(meta, owner, mine, swap(mine), own_roots(meta, mine))


def solution(mesh):
    fine = Mesh(mesh.devices.reshape(4, 4, 2, 4), ("z", "y", "c", "x"))
    dp = ("z", "y", "c")
    return jax.shard_map(
        body,
        mesh=fine,
        in_specs=(P(dp, None, None, "x"), P(), P(dp, "x", None), P()),
        out_specs=(P(dp, "x", None), P(None, "x", None)),
        check_vma=False,
    )
```

```python
import jax
import jax.numpy as jnp
from jax import lax
from jax.experimental import pallas as pl
from jax.experimental.pallas import tpu as pltpu
from jax.sharding import Mesh, PartitionSpec as P

ITERS = 2
K = 256
Q = 64
L = 128
STEP = 8
PART = 2
SWAP = K + 32
SENT = K + 16
SEND = SENT + Q
PIECE = K + 8
f32 = jnp.float32
bf16 = jnp.bfloat16
HI = lax.Precision.HIGHEST


def iotas(rows):
    row = lax.broadcasted_iota(jnp.int32, (rows, L), 0)
    lane = lax.broadcasted_iota(jnp.int32, (rows, L), 1)
    return row, lane


def pick_masks(m):
    row, lane = iotas(Q)
    odd = m % 2
    below = ((lane - Q * odd) < row).astype(jnp.int32)
    right = (lane >= Q).astype(jnp.int32)
    from_diag = jnp.maximum(right, below) * (1 - odd) + right * below * odd
    return from_diag > 0, lane == row + Q * odd


def pack(rows, m, masks):
    t0, t1 = rows[:, :L], rows[:, L:]
    if isinstance(m, int):
        diag_tile, other = (t0, t1) if m < 2 else (t1, t0)
    else:
        diag_tile = jnp.where(m < 2, t0, t1)
        other = jnp.where(m < 2, t1, t0)
    from_diag, on_diag = masks
    packed = jnp.where(from_diag, diag_tile, other)
    spread = jnp.where(on_diag, diag_tile, 0.0)
    diag = spread[:8]
    for i in range(8, Q, 8):
        diag = diag + spread[i:i + 8]
    return packed, diag


def split_diag(d):
    hi = d.astype(bf16).astype(f32)
    return (hi + pltpu.roll(d - hi, Q, 1)).astype(bf16)


def gram_of(g_refs, k):
    g = g_refs[k // PART][0, k % PART]
    return lax.dot_general(g, g, (((1,), (1,)), ((), ())), preferred_element_type=f32)


def gram_pack(gram, out_ref, k, masks, dtype):
    diags = []
    for m in range(4):
        packed, d = pack(gram[Q * m:Q * (m + 1)], m, masks[m])
        out_ref[k, Q * m:Q * (m + 1), :] = packed.astype(dtype)
        diags.append(d)
    return jnp.concatenate(diags, axis=0)


def gram_send_kernel(meta, *refs):
    g_refs, out_ref = refs[:-1], refs[-1]
    masks = [pick_masks(m) for m in range(4)]
    for k in range(STEP):
        out_ref[k, K:, :] = split_diag(gram_pack(gram_of(g_refs, k), out_ref, k, masks, bf16))


def rank_of(owner_ref, f, o):
    return lax.fori_loop(0, f, lambda g, n: n + (owner_ref[g] == o).astype(jnp.int32), jnp.int32(0))


def gram_keep_kernel(meta, *refs):
    g_refs, out_ref = refs[:-1], refs[-1]
    masks = [pick_masks(m) for m in range(4)]
    for k in range(STEP):
        out_ref[k, K:, :] = gram_pack(gram_of(g_refs, k), out_ref, k, masks, f32)


def merge_kernel(scale, meta, owner_ref, own_ref, got_ref, mine, theirs, out_ref, parts, diags):
    x, c, zy = meta[0], meta[1], meta[2]
    quarter = pl.ds(pl.multiple_of(Q * x, Q), Q)
    owners = [owner_ref[c * 16 + j] for j in range(16)]
    row, lane = iotas(32)
    odd = (row // 8) % 2
    own_half = (lane >= Q * odd) & (lane < Q * odd + Q)
    for j in range(16):
        out_ref[j, :K, :] = ((own_ref[j, :K, :] + got_ref[j, :K, :].astype(f32)) * scale).astype(bf16)
        got = got_ref[j, K:, :].astype(f32)
        got = jnp.where(own_half, got + pltpu.roll(got, Q, 1), 0.0)
        diags[j] = (own_ref[j, K:, :] + got) * scale
        parts[j] = (own_ref[j, quarter, :] + got_ref[j, quarter, :].astype(f32)) * scale
    for j in range(16):
        @pl.when(owners[j] // 2 == zy)
        def _(j=j):
            o = owners[j]
            r = rank_of(owner_ref, c * 16 + j, o)
            pick = jnp.where(o % 2 == c, 1.0, 0.0)
            old = mine[r] * pick + theirs[r] * (1.0 - pick)
            packed, d = pack(old, x, pick_masks(x))
            parts[j] += packed
            diags[j, pl.ds(pl.multiple_of(8 * x, 8), 8), :] += d

    last, _ = iotas(16)
    for j in range(16):
        high = parts[j].astype(bf16)
        out_ref[j, quarter, :] = high
        out_ref[j, SENT:, :] = (parts[j] - high.astype(f32)).astype(bf16)
        diag = jnp.zeros((16, L), f32)
        for m in range(4):
            diag = jnp.where(last == m, jnp.sum(diags[j, 8 * m:8 * m + 8, :], axis=0, keepdims=True), diag)
        out_ref[j, K:SENT, :] = split_diag(diag)


def params(mib):
    return pltpu.CompilerParams(vmem_limit_bytes=mib * 2**20)


GRAM_COST = pl.CostEstimate(flops=32 * K * K * 512, bytes_accessed=16 * K * 512 * 2 + 2**21, transcendentals=0)


def gram_call(kernel, core_of, dtype, name, meta, grads):
    parts = STEP // PART
    per = 16 // PART

    def part(p):
        return pl.BlockSpec((1, PART, K, 512), lambda i, meta: (0, core_of(meta[1]) * per + i * parts + p, 0, 0))

    return pl.pallas_call(
        kernel,
        grid_spec=pltpu.PrefetchScalarGridSpec(
            num_scalar_prefetch=1,
            grid=(16 // STEP,),
            in_specs=[part(p) for p in range(parts)],
            out_specs=pl.BlockSpec((STEP, SWAP, L), lambda i, meta: (i, 0, 0)),
        ),
        out_shape=jax.ShapeDtypeStruct((16, SWAP, L), dtype),
        compiler_params=params(48),
        cost_estimate=GRAM_COST,
        name=name,
    )(meta, *([grads] * parts))


def merge(scale, meta, owner, own, got, mine, theirs):
    whole = pl.BlockSpec((16, SWAP, L), lambda i, *_: (0, 0, 0))
    old = pl.BlockSpec((3, Q, K), lambda i, *_: (0, 0, 0))

    def kernel(*refs):
        merge_kernel(scale, *refs)

    return pl.pallas_call(
        kernel,
        grid_spec=pltpu.PrefetchScalarGridSpec(
            num_scalar_prefetch=2,
            grid=(1,),
            in_specs=[whole, whole, old, old],
            out_specs=pl.BlockSpec((16, SEND, L), lambda i, *_: (0, 0, 0)),
            scratch_shapes=[pltpu.VMEM((16, Q, L), f32), pltpu.VMEM((16, 32, L), f32)],
        ),
        out_shape=jax.ShapeDtypeStruct((16, SEND, L), bf16),
        compiler_params=params(24),
        cost_estimate=pl.CostEstimate(flops=2**20, bytes_accessed=2**22, transcendentals=0),
        name="merge",
    )(meta, owner, own, got, mine, theirs)


def plane_sum_kernel(arrived, out_ref):
    for m in range(4):
        rows = slice(Q * m, Q * (m + 1))
        total = arrived[0, rows, :].astype(f32)
        for j in range(1, 16):
            total = total + arrived[j, rows, :].astype(f32)
        for y in range(4):
            total = total + arrived[4 * m + y, SENT:, :].astype(f32)
        out_ref[rows, :] = total
    total = arrived[0, K:SENT, :].astype(f32)
    for j in range(1, 16):
        total = total + arrived[j, K:SENT, :].astype(f32)
    out_ref[K:, :] = total[:8]


def plane_sum(arrived):
    return pl.pallas_call(
        plane_sum_kernel,
        grid=(1,),
        in_specs=[pl.BlockSpec((16, SEND, L), lambda i: (0, 0, 0))],
        out_specs=pl.BlockSpec((PIECE, L), lambda i: (0, 0)),
        out_shape=jax.ShapeDtypeStruct((PIECE, L), f32),
        compiler_params=params(16),
        name="plane_sum",
    )(arrived)


def unpack(total, half):
    row, lane = iotas(Q)
    ends = total[K:]
    ends = ends + pltpu.roll(ends, Q, 1)
    for m in range(4):
        odd = m % 2
        part = total[Q * m:Q * (m + 1)]
        below = (lane - Q * odd) < row
        equal = lane == row + Q * odd
        right = lane >= Q
        from_diag = (right | below) if odd == 0 else (right & below)
        diag_tile = jnp.where(from_diag, part, 0.0)
        other = jnp.where(from_diag, 0.0, part)
        if m >= 2:
            other = jnp.where(equal, 0.0, other)
        diag_tile = diag_tile + jnp.where(equal, 0.5 * ends[m:m + 1], 0.0)
        tiles = (diag_tile, other) if m < 2 else (other, diag_tile)
        half[Q * m:Q * (m + 1), :L] = tiles[0]
        half[Q * m:Q * (m + 1), L:] = tiles[1]
    h = half[...]
    return h + h.T


def halves(a):
    high = a.astype(bf16)
    return high, (a - high.astype(f32)).astype(bf16)


def mm(a, b):
    (ah, al), (bh, bl) = halves(a), halves(b)
    dot = lambda u, v: jnp.dot(u, v, preferred_element_type=f32)
    return (dot(al, bh) + dot(ah, bl)) + dot(ah, bh)


def fourth_kernel(meta, root_ref, out_ref, copy_ref):
    r = root_ref[0]
    copy_ref[...] = r
    square = jnp.dot(r, r, preferred_element_type=f32)
    out_ref[...] = mm(square, square)


def fourth(meta, prev_roots):
    whole = pl.BlockSpec((K, K), lambda i, meta: (0, 0))
    return pl.pallas_call(
        fourth_kernel,
        grid_spec=pltpu.PrefetchScalarGridSpec(
            num_scalar_prefetch=1,
            grid=(1,),
            in_specs=[pl.BlockSpec((1, K, K), lambda i, meta: (meta[3], 0, 0))],
            out_specs=[whole, whole],
        ),
        out_shape=[jax.ShapeDtypeStruct((K, K), f32), jax.ShapeDtypeStruct((K, K), bf16)],
        compiler_params=params(8),
        cost_estimate=pl.CostEstimate(flops=14 * K**3, bytes_accessed=6 * K * K, transcendentals=0),
        name="fourth",
    )(meta, prev_roots)


def newton_kernel(meta, root_ref, fourth_ref, *refs):
    pieces, (out_ref, held, half) = refs[:4], refs[4:]
    z = meta[4]
    for s in range(4):
        held[lax.rem(z - s + 4, 4)] = pieces[s][...]
    factor = unpack(((held[0] + held[1]) + held[2]) + held[3], half)
    high = factor.astype(bf16)
    low = (factor - high.astype(f32)).astype(bf16)
    row = lax.broadcasted_iota(jnp.int32, (K, K), 0)
    col = lax.broadcasted_iota(jnp.int32, (K, K), 1)
    five = jnp.where(row == col, 5.0, 0.0)
    coupled = mm(fourth_ref[...], factor)
    root = root_ref[...].astype(f32)
    for iteration in range(ITERS):
        update = (five - coupled) * 0.25
        root = mm(root, update)
        if iteration + 1 < ITERS:
            square = mm(update, update)
            coupled = mm(mm(square, square), coupled)
    root = root.astype(bf16)
    for j in range(16):
        rows = slice(Q * (j // 4), Q * (j // 4 + 1))
        out_ref[j, :Q] = root[rows]
        out_ref[j, Q:2 * Q] = high[rows]
        out_ref[j, 2 * Q:] = low[rows]


def newton(meta, root, power, pieces):
    whole = pl.BlockSpec((K, K), lambda i, meta: (0, 0))
    piece = pl.BlockSpec((PIECE, L), lambda i, meta: (0, 0))
    return pl.pallas_call(
        newton_kernel,
        grid_spec=pltpu.PrefetchScalarGridSpec(
            num_scalar_prefetch=1,
            grid=(1,),
            in_specs=[whole, whole] + [piece] * 4,
            out_specs=pl.BlockSpec((16, 3 * Q, K), lambda i, meta: (0, 0, 0)),
            scratch_shapes=[pltpu.VMEM((4, PIECE, L), f32), pltpu.VMEM((K, K), f32)],
        ),
        out_shape=jax.ShapeDtypeStruct((16, 3 * Q, K), bf16),
        compiler_params=params(16),
        cost_estimate=pl.CostEstimate(flops=60 * K**3, bytes_accessed=2**21, transcendentals=0),
        name="newton",
    )(meta, root, power, *pieces)


ANY = pl.BlockSpec(memory_space=pl.ANY)
ROOTS = jax.ShapeDtypeStruct((32 * Q, K), bf16)
SIBLING = 16 * Q + 3 * 2 * Q


def own_roots_kernel(meta, mine, roots_ref, sems):
    base = 16 * Q * meta[1]
    copies = [
        pltpu.make_async_copy(mine.at[j, pl.ds(0, Q), :], roots_ref.at[pl.ds(base + Q * j, Q)], sems.at[j])
        for j in range(16)
    ]
    for copy in copies:
        copy.start()
    for copy in copies:
        copy.wait()


ARRIVED = pl.BlockSpec((16, 3 * Q, K), lambda i, *_: (0, 0, 0))


def own_roots(meta, mine):
    return pl.pallas_call(
        own_roots_kernel,
        grid_spec=pltpu.PrefetchScalarGridSpec(
            num_scalar_prefetch=1,
            grid=(1,),
            in_specs=[ARRIVED],
            out_specs=ANY,
            scratch_shapes=[pltpu.SemaphoreType.DMA((16,))],
        ),
        out_shape=ROOTS,
        compiler_params=params(16),
        cost_estimate=pl.CostEstimate(flops=0, bytes_accessed=2**20, transcendentals=0),
        name="own_roots",
    )(meta, mine)


def slots_of(owner_ref, target):
    count = jnp.int32(0)
    slot = [jnp.int32(0)] * 3
    for f in range(32):
        hit = owner_ref[f] == target
        slot = [jnp.where(hit & (count == n), f, slot[n]) for n in range(3)]
        count = count + hit.astype(jnp.int32)
    return count, slot


def select_kernel(meta, owner_ref, mine, out_ref):
    c, zy = meta[1], meta[2]
    count, slot = slots_of(owner_ref, 2 * zy + 1 - c)
    for j in range(16):
        out_ref[Q * j:Q * (j + 1), :] = mine[j, :Q, :]
    for n in range(3):
        rows = slice(16 * Q + 2 * Q * n, 16 * Q + 2 * Q * (n + 1))
        here = (n < count) & (slot[n] // 16 == c)

        @pl.when(here)
        def _(n=n, rows=rows):
            out_ref[rows, :] = mine[lax.rem(slot[n], 16), Q:, :]

        @pl.when(jnp.logical_not(here))
        def _(rows=rows):
            out_ref[rows, :] = jnp.zeros((2 * Q, K), bf16)


def select(meta, owner, mine):
    return pl.pallas_call(
        select_kernel,
        grid_spec=pltpu.PrefetchScalarGridSpec(
            num_scalar_prefetch=2,
            grid=(1,),
            in_specs=[ARRIVED],
            out_specs=pl.BlockSpec((SIBLING, K), lambda i, *_: (0, 0)),
        ),
        out_shape=jax.ShapeDtypeStruct((SIBLING, K), bf16),
        compiler_params=params(16),
        name="select",
    )(meta, owner, mine)


def finish_kernel(meta, owner_ref, mine, theirs, before, stats_ref, roots_ref, held, sems, slot_sems):
    c, zy = meta[1], meta[2]
    copies = [
        pltpu.make_async_copy(
            theirs.at[pl.ds(4 * Q * i, 4 * Q), :], roots_ref.at[pl.ds(16 * Q * (1 - c) + 4 * Q * i, 4 * Q)], sems.at[i]
        )
        for i in range(4)
    ]
    for copy in copies:
        copy.start()
    count, slot = slots_of(owner_ref, 2 * zy + c)
    out = [pltpu.make_async_copy(held.at[n], stats_ref.at[n], slot_sems.at[n]) for n in range(3)]
    for n in range(3):
        near = slot[n] // 16 == c
        at = 16 * Q + 2 * Q * n

        @pl.when((n < count) & near)
        def _(n=n):
            j = lax.rem(slot[n], 16)
            held[n] = mine[j, Q:2 * Q, :].astype(f32) + mine[j, 2 * Q:, :].astype(f32)

        @pl.when((n < count) & jnp.logical_not(near))
        def _(n=n, at=at):
            held[n] = theirs[at:at + Q, :].astype(f32) + theirs[at + Q:at + 2 * Q, :].astype(f32)

        @pl.when(n >= count)
        def _(n=n):
            held[n] = jnp.zeros((Q, K), f32)

        out[n].start()
    for copy in out + copies:
        copy.wait()


def finish(meta, owner, mine, theirs, roots):
    return pl.pallas_call(
        finish_kernel,
        grid_spec=pltpu.PrefetchScalarGridSpec(
            num_scalar_prefetch=2,
            grid=(1,),
            in_specs=[ARRIVED, pl.BlockSpec((SIBLING, K), lambda i, *_: (0, 0)), ANY],
            out_specs=[ANY, ANY],
            scratch_shapes=[
                pltpu.VMEM((3, Q, K), f32),
                pltpu.SemaphoreType.DMA((4,)),
                pltpu.SemaphoreType.DMA((3,)),
            ],
        ),
        out_shape=[jax.ShapeDtypeStruct((3, Q, K), f32), ROOTS],
        input_output_aliases={4: 1},
        compiler_params=params(16),
        name="finish",
    )(meta, owner, mine, theirs, roots)


def swap(a):
    return lax.ppermute(a, "c", [(0, 1), (1, 0)])


def turn(a, s):
    return lax.ppermute(a, "z", [(i, (i + s) % 4) for i in range(4)])


def body(grads, owner, stats_old, prev_roots):
    z, y, c, x = (lax.axis_index(a) for a in ("z", "y", "c", "x"))
    scale = 1.0 / (32 * 2048)
    meta = jnp.stack([x, c, z * 4 + y, c * 16 + x * 4 + y, z]).astype(jnp.int32)
    their_old = swap(stats_old)
    got = swap(gram_call(gram_send_kernel, lambda core: 1 - core, bf16, "gram_send", meta, grads))
    own = gram_call(gram_keep_kernel, lambda core: core, f32, "gram_keep", meta, grads)
    outgoing = merge(scale, meta, owner, own, got, stats_old, their_old)
    arrived = lax.all_to_all(outgoing, ("x", "y"), 0, 0, tiled=True)
    piece = plane_sum(arrived)
    power, root = fourth(meta, prev_roots)
    pieces = [piece] + [turn(piece, s) for s in (1, 2, 3)]
    mine = lax.all_to_all(newton(meta, root, power, pieces), ("x", "y"), 0, 0, tiled=True)
    theirs = swap(select(meta, owner, mine))
    stats_new, roots = finish(meta, owner, mine, theirs, own_roots(meta, mine))
    return stats_new, roots.reshape(32, Q, K)


def solution(mesh):
    fine = Mesh(mesh.devices.reshape(4, 4, 2, 4), ("z", "y", "c", "x"))
    dp = ("z", "y", "c")
    return jax.shard_map(
        body,
        mesh=fine,
        in_specs=(P(dp, None, None, "x"), P(), P(dp, "x", None), P()),
        out_specs=(P(dp, "x", None), P(None, "x", None)),
        check_vma=False,
    )
```

```python
import jax
import jax.numpy as jnp
from jax import lax
from jax.experimental import pallas as pl
from jax.experimental.pallas import tpu as pltpu
from jax.sharding import Mesh, PartitionSpec as P

ITERS = 2
K = 256
Q = 64
T = 16
L = 128
STEP = 8
PART = 2
SWAP = K + 32
SENT = K + 16
SEND = SENT + Q
PIECE = K + 8
f32 = jnp.float32
bf16 = jnp.bfloat16
ANY = pl.BlockSpec(memory_space=pl.ANY)


def iotas(rows):
    row = lax.broadcasted_iota(jnp.int32, (rows, L), 0)
    lane = lax.broadcasted_iota(jnp.int32, (rows, L), 1)
    return row, lane


def pick_masks(m):
    row, lane = iotas(Q)
    odd = m % 2
    below = ((lane - Q * odd) < row).astype(jnp.int32)
    right = (lane >= Q).astype(jnp.int32)
    from_diag = jnp.maximum(right, below) * (1 - odd) + right * below * odd
    return from_diag > 0, lane == row + Q * odd


def pack(rows, m, masks):
    t0, t1 = rows[:, :L], rows[:, L:]
    if isinstance(m, int):
        diag_tile, other = (t0, t1) if m < 2 else (t1, t0)
    else:
        diag_tile = jnp.where(m < 2, t0, t1)
        other = jnp.where(m < 2, t1, t0)
    from_diag, on_diag = masks
    packed = jnp.where(from_diag, diag_tile, other)
    spread = jnp.where(on_diag, diag_tile, 0.0)
    diag = spread[:8]
    for i in range(8, Q, 8):
        diag = diag + spread[i:i + 8]
    return packed, diag


def split_diag(d):
    hi = d.astype(bf16).astype(f32)
    return (hi + pltpu.roll(d - hi, Q, 1)).astype(bf16)


def gram_of(g_refs, k):
    g = g_refs[k // PART][0, k % PART]
    return lax.dot_general(g, g, (((1,), (1,)), ((), ())), preferred_element_type=f32)


def gram_pack(gram, out_ref, k, masks, dtype):
    diags = []
    for m in range(4):
        packed, d = pack(gram[Q * m:Q * (m + 1)], m, masks[m])
        out_ref[k, Q * m:Q * (m + 1), :] = packed.astype(dtype)
        diags.append(d)
    return jnp.concatenate(diags, axis=0)


def gram_send_kernel(meta, *refs):
    g_refs, out_ref = refs[:-1], refs[-1]
    masks = [pick_masks(m) for m in range(4)]
    for k in range(STEP):
        out_ref[k, K:, :] = split_diag(gram_pack(gram_of(g_refs, k), out_ref, k, masks, bf16))


def rank_of(owner_ref, f, o):
    return lax.fori_loop(0, f, lambda g, n: n + (owner_ref[g] == o).astype(jnp.int32), jnp.int32(0))


def gram_keep_kernel(meta, *refs):
    g_refs, out_ref = refs[:-1], refs[-1]
    masks = [pick_masks(m) for m in range(4)]
    for k in range(STEP):
        out_ref[k, K:, :] = gram_pack(gram_of(g_refs, k), out_ref, k, masks, f32)


def merge_kernel(scale, meta, owner_ref, own_ref, got_ref, mine, theirs, out_ref, parts, diags):
    x, c, zy = meta[0], meta[1], meta[2]
    quarter = pl.ds(pl.multiple_of(Q * x, Q), Q)
    owners = [owner_ref[c * 16 + j] for j in range(16)]
    row, lane = iotas(32)
    odd = (row // 8) % 2
    own_half = (lane >= Q * odd) & (lane < Q * odd + Q)
    for j in range(16):
        out_ref[j, :K, :] = ((own_ref[j, :K, :] + got_ref[j, :K, :].astype(f32)) * scale).astype(bf16)
        got = got_ref[j, K:, :].astype(f32)
        got = jnp.where(own_half, got + pltpu.roll(got, Q, 1), 0.0)
        diags[j] = (own_ref[j, K:, :] + got) * scale
        parts[j] = (own_ref[j, quarter, :] + got_ref[j, quarter, :].astype(f32)) * scale
    for j in range(16):
        @pl.when(owners[j] // 2 == zy)
        def _(j=j):
            o = owners[j]
            r = rank_of(owner_ref, c * 16 + j, o)
            pick = jnp.where(o % 2 == c, 1.0, 0.0)
            old = mine[r] * pick + theirs[r] * (1.0 - pick)
            packed, d = pack(old, x, pick_masks(x))
            parts[j] += packed
            diags[j, pl.ds(pl.multiple_of(8 * x, 8), 8), :] += d

    last, _ = iotas(16)
    for j in range(16):
        high = parts[j].astype(bf16)
        out_ref[j, quarter, :] = high
        out_ref[j, SENT:, :] = (parts[j] - high.astype(f32)).astype(bf16)
        diag = jnp.zeros((16, L), f32)
        for m in range(4):
            diag = jnp.where(last == m, jnp.sum(diags[j, 8 * m:8 * m + 8, :], axis=0, keepdims=True), diag)
        out_ref[j, K:SENT, :] = split_diag(diag)


def params(mib):
    return pltpu.CompilerParams(vmem_limit_bytes=mib * 2**20)


GRAM_COST = pl.CostEstimate(flops=32 * K * K * 512, bytes_accessed=16 * K * 512 * 2 + 2**21, transcendentals=0)


def gram_call(kernel, core_of, dtype, name, meta, grads):
    parts = STEP // PART
    per = 16 // PART

    def part(p):
        return pl.BlockSpec((1, PART, K, 512), lambda i, meta: (0, core_of(meta[1]) * per + i * parts + p, 0, 0))

    return pl.pallas_call(
        kernel,
        grid_spec=pltpu.PrefetchScalarGridSpec(
            num_scalar_prefetch=1,
            grid=(16 // STEP,),
            in_specs=[part(p) for p in range(parts)],
            out_specs=pl.BlockSpec((STEP, SWAP, L), lambda i, meta: (i, 0, 0)),
        ),
        out_shape=jax.ShapeDtypeStruct((16, SWAP, L), dtype),
        compiler_params=params(48),
        cost_estimate=GRAM_COST,
        name=name,
    )(meta, *([grads] * parts))


def merge(scale, meta, owner, own, got, mine, theirs):
    whole = pl.BlockSpec((16, SWAP, L), lambda i, *_: (0, 0, 0))
    old = pl.BlockSpec((3, Q, K), lambda i, *_: (0, 0, 0))

    def kernel(*refs):
        merge_kernel(scale, *refs)

    return pl.pallas_call(
        kernel,
        grid_spec=pltpu.PrefetchScalarGridSpec(
            num_scalar_prefetch=2,
            grid=(1,),
            in_specs=[whole, whole, old, old],
            out_specs=pl.BlockSpec((16, SEND, L), lambda i, *_: (0, 0, 0)),
            scratch_shapes=[pltpu.VMEM((16, Q, L), f32), pltpu.VMEM((16, 32, L), f32)],
        ),
        out_shape=jax.ShapeDtypeStruct((16, SEND, L), bf16),
        compiler_params=params(24),
        cost_estimate=pl.CostEstimate(flops=2**20, bytes_accessed=2**22, transcendentals=0),
        name="merge",
    )(meta, owner, own, got, mine, theirs)


def plane_sum_kernel(arrived, out_ref):
    for m in range(4):
        rows = slice(Q * m, Q * (m + 1))
        total = arrived[0, rows, :].astype(f32)
        for j in range(1, 16):
            total = total + arrived[j, rows, :].astype(f32)
        for y in range(4):
            total = total + arrived[4 * m + y, SENT:, :].astype(f32)
        out_ref[rows, :] = total
    total = arrived[0, K:SENT, :].astype(f32)
    for j in range(1, 16):
        total = total + arrived[j, K:SENT, :].astype(f32)
    out_ref[K:, :] = total[:8]


def plane_sum(arrived):
    return pl.pallas_call(
        plane_sum_kernel,
        grid=(1,),
        in_specs=[pl.BlockSpec((16, SEND, L), lambda i: (0, 0, 0))],
        out_specs=pl.BlockSpec((PIECE, L), lambda i: (0, 0)),
        out_shape=jax.ShapeDtypeStruct((PIECE, L), f32),
        compiler_params=params(16),
        name="plane_sum",
    )(arrived)


def unpack(total, half):
    row, lane = iotas(Q)
    ends = total[K:]
    ends = ends + pltpu.roll(ends, Q, 1)
    for m in range(4):
        odd = m % 2
        part = total[Q * m:Q * (m + 1)]
        below = (lane - Q * odd) < row
        equal = lane == row + Q * odd
        right = lane >= Q
        from_diag = (right | below) if odd == 0 else (right & below)
        diag_tile = jnp.where(from_diag, part, 0.0)
        other = jnp.where(from_diag, 0.0, part)
        if m >= 2:
            other = jnp.where(equal, 0.0, other)
        diag_tile = diag_tile + jnp.where(equal, 0.5 * ends[m:m + 1], 0.0)
        tiles = (diag_tile, other) if m < 2 else (other, diag_tile)
        half[Q * m:Q * (m + 1), :L] = tiles[0]
        half[Q * m:Q * (m + 1), L:] = tiles[1]
    h = half[...]
    return h + h.T


def halves(a):
    high = a.astype(bf16)
    return high, (a - high.astype(f32)).astype(bf16)


def mm(a, b):
    (ah, al), (bh, bl) = halves(a), halves(b)
    dot = lambda u, v: jnp.dot(u, v, preferred_element_type=f32)
    return (dot(al, bh) + dot(ah, bl)) + dot(ah, bh)


def fourth_kernel(meta, root_ref, out_ref, copy_ref):
    r = root_ref[0]
    copy_ref[...] = r
    square = jnp.dot(r, r, preferred_element_type=f32)
    out_ref[...] = mm(square, square)


def fourth(meta, prev_roots):
    whole = pl.BlockSpec((K, K), lambda i, meta: (0, 0))
    return pl.pallas_call(
        fourth_kernel,
        grid_spec=pltpu.PrefetchScalarGridSpec(
            num_scalar_prefetch=1,
            grid=(1,),
            in_specs=[pl.BlockSpec((1, K, K), lambda i, meta: (meta[3], 0, 0))],
            out_specs=[whole, whole],
        ),
        out_shape=[jax.ShapeDtypeStruct((K, K), f32), jax.ShapeDtypeStruct((K, K), bf16)],
        compiler_params=params(8),
        cost_estimate=pl.CostEstimate(flops=14 * K**3, bytes_accessed=6 * K * K, transcendentals=0),
        name="fourth",
    )(meta, prev_roots)


def newton_kernel(meta, root_ref, fourth_ref, *refs):
    pieces, (out_ref, held, half) = refs[:4], refs[4:]
    z = meta[4]
    for s in range(4):
        held[lax.rem(z - s + 4, 4)] = pieces[s][...]
    factor = unpack(((held[0] + held[1]) + held[2]) + held[3], half)
    half[...] = factor
    row = lax.broadcasted_iota(jnp.int32, (K, K), 0)
    col = lax.broadcasted_iota(jnp.int32, (K, K), 1)
    five = jnp.where(row == col, 5.0, 0.0)
    coupled = mm(fourth_ref[...], factor)
    root = root_ref[...].astype(f32)
    for iteration in range(ITERS):
        update = (five - coupled) * 0.25
        root = mm(root, update)
        if iteration + 1 < ITERS:
            square = mm(update, update)
            coupled = mm(mm(square, square), coupled)
    root = root.astype(bf16)
    for j in range(16):
        rows = slice(Q * (j // 4), Q * (j // 4 + 1))
        out_ref[j, :Q] = root[rows]
        part = half[pl.ds(pl.multiple_of(Q * (j // 4) + T * z, T), T), :]
        high = part.astype(bf16)
        out_ref[j, Q:Q + T] = high
        out_ref[j, Q + T:] = (part - high.astype(f32)).astype(bf16)


def newton(meta, root, power, pieces):
    whole = pl.BlockSpec((K, K), lambda i, meta: (0, 0))
    piece = pl.BlockSpec((PIECE, L), lambda i, meta: (0, 0))
    return pl.pallas_call(
        newton_kernel,
        grid_spec=pltpu.PrefetchScalarGridSpec(
            num_scalar_prefetch=1,
            grid=(1,),
            in_specs=[whole, whole] + [piece] * 4,
            out_specs=pl.BlockSpec((16, Q + 2 * T, K), lambda i, meta: (0, 0, 0)),
            scratch_shapes=[pltpu.VMEM((4, PIECE, L), f32), pltpu.VMEM((K, K), f32)],
        ),
        out_shape=jax.ShapeDtypeStruct((16, Q + 2 * T, K), bf16),
        compiler_params=params(16),
        cost_estimate=pl.CostEstimate(flops=60 * K**3, bytes_accessed=2**21, transcendentals=0),
        name="newton",
    )(meta, root, power, *pieces)


ARRIVED = pl.BlockSpec((16, Q + 2 * T, K), lambda i, *_: (0, 0, 0))
OWNED = jax.ShapeDtypeStruct((4, 3, T, K), f32)
SLICE = jax.ShapeDtypeStruct((3, T, K), f32)


def pick_kernel(meta, owner_ref, mine, keep_ref, give_ref):
    c, y = meta[1], lax.rem(meta[2], 4)
    keep_ref[...] = jnp.zeros(keep_ref.shape, f32)
    give_ref[...] = jnp.zeros(give_ref.shape, f32)
    first = [owner_ref[g] for g in range(16)]
    own = [owner_ref[16 * c + g] for g in range(16)]
    for j in range(16):
        o = own[j]

        @pl.when(lax.rem(o // 2, 4) == y)
        def _(j=j, o=o):
            r = jnp.int32(0)
            for g in range(16):
                r = r + (first[g] == o).astype(jnp.int32)
            r = r * c
            for g in range(j):
                r = r + (own[g] == o).astype(jnp.int32)
            rows = mine[j, Q:Q + T, :].astype(f32) + mine[j, Q + T:, :].astype(f32)

            @pl.when(lax.rem(o, 2) == c)
            def _():
                keep_ref[o // 8, r] = rows

            @pl.when(lax.rem(o, 2) != c)
            def _():
                give_ref[o // 8, r] = rows


def pick(meta, owner, mine):
    block = pl.BlockSpec((4, 3, T, K), lambda i, *_: (0, 0, 0, 0))
    return pl.pallas_call(
        pick_kernel,
        grid_spec=pltpu.PrefetchScalarGridSpec(
            num_scalar_prefetch=2, grid=(1,), in_specs=[ARRIVED], out_specs=[block, block]
        ),
        out_shape=[OWNED, OWNED],
        compiler_params=params(12),
        name="pick",
    )(meta, owner, mine)


def spread_kernel(meta, keep, got, *out):
    z = meta[4]
    for s in range(4):
        plane = lax.rem(z + s, 4)
        out[s][...] = keep[plane] + got[plane]


def spread(meta, keep, got):
    block = pl.BlockSpec((4, 3, T, K), lambda i, *_: (0, 0, 0, 0))
    piece = pl.BlockSpec((3, T, K), lambda i, *_: (0, 0, 0))
    return pl.pallas_call(
        spread_kernel,
        grid_spec=pltpu.PrefetchScalarGridSpec(
            num_scalar_prefetch=1, grid=(1,), in_specs=[block, block], out_specs=[piece] * 4
        ),
        out_shape=[SLICE] * 4,
        compiler_params=params(12),
        name="spread",
    )(meta, keep, got)


def stats_kernel(meta, *refs):
    pieces, out_ref = refs[:4], refs[4]
    for s in range(4):
        rows = pl.ds(pl.multiple_of(T * lax.rem(meta[4] - s + 4, 4), T), T)
        out_ref[:, rows, :] = pieces[s][...]


def stats(meta, pieces):
    piece = pl.BlockSpec((3, T, K), lambda i, *_: (0, 0, 0))
    return pl.pallas_call(
        stats_kernel,
        grid_spec=pltpu.PrefetchScalarGridSpec(
            num_scalar_prefetch=1,
            grid=(1,),
            in_specs=[piece] * 4,
            out_specs=pl.BlockSpec((3, Q, K), lambda i, *_: (0, 0, 0)),
        ),
        out_shape=jax.ShapeDtypeStruct((3, Q, K), f32),
        compiler_params=params(12),
        name="stats",
    )(meta, *pieces)


def near_roots_kernel(mine, out_ref):
    out_ref[...] = mine[:, :Q, :]


def near_roots(mine):
    return pl.pallas_call(
        near_roots_kernel,
        grid=(1,),
        in_specs=[ARRIVED],
        out_specs=pl.BlockSpec((16, Q, K), lambda i: (0, 0, 0)),
        out_shape=jax.ShapeDtypeStruct((16, Q, K), bf16),
        compiler_params=params(12),
        name="near_roots",
    )(mine)


def all_roots_kernel(meta, near, far, out_ref, sems):
    c = meta[1]
    copies = []
    for i in range(4):
        part = pl.ds(4 * i, 4)
        copies.append(pltpu.make_async_copy(near.at[part], out_ref.at[pl.ds(16 * c + 4 * i, 4)], sems.at[i]))
        copies.append(pltpu.make_async_copy(far.at[part], out_ref.at[pl.ds(16 * (1 - c) + 4 * i, 4)], sems.at[4 + i]))
    for copy in copies:
        copy.start()
    for copy in copies:
        copy.wait()


def all_roots(meta, near, far):
    block = pl.BlockSpec((16, Q, K), lambda i, *_: (0, 0, 0))
    return pl.pallas_call(
        all_roots_kernel,
        grid_spec=pltpu.PrefetchScalarGridSpec(
            num_scalar_prefetch=1,
            grid=(1,),
            in_specs=[block, block],
            out_specs=ANY,
            scratch_shapes=[pltpu.SemaphoreType.DMA((8,))],
        ),
        out_shape=jax.ShapeDtypeStruct((32, Q, K), bf16),
        compiler_params=params(12),
        cost_estimate=pl.CostEstimate(flops=0, bytes_accessed=2**21, transcendentals=0),
        name="all_roots",
    )(meta, near, far)


def swap(a):
    return lax.ppermute(a, "c", [(0, 1), (1, 0)])


def turn(a, s):
    return lax.ppermute(a, "z", [(i, (i + s) % 4) for i in range(4)])


def body(grads, owner, stats_old, prev_roots):
    z, y, c, x = (lax.axis_index(a) for a in ("z", "y", "c", "x"))
    scale = 1.0 / (32 * 2048)
    meta = jnp.stack([x, c, z * 4 + y, c * 16 + x * 4 + y, z]).astype(jnp.int32)
    their_old = swap(stats_old)
    got = swap(gram_call(gram_send_kernel, lambda core: 1 - core, bf16, "gram_send", meta, grads))
    own = gram_call(gram_keep_kernel, lambda core: core, f32, "gram_keep", meta, grads)
    outgoing = merge(scale, meta, owner, own, got, stats_old, their_old)
    arrived = lax.all_to_all(outgoing, ("x", "y"), 0, 0, tiled=True)
    piece = plane_sum(arrived)
    power, root = fourth(meta, prev_roots)
    pieces = [piece] + [turn(piece, s) for s in (1, 2, 3)]
    mine = lax.all_to_all(newton(meta, root, power, pieces), ("x", "y"), 0, 0, tiled=True)
    keep, give = pick(meta, owner, mine)
    parts = spread(meta, keep, swap(give))
    arrived_parts = [parts[0]] + [turn(parts[s], s) for s in (1, 2, 3)]
    near = near_roots(lax.optimization_barrier((mine, parts[0]))[0])
    roots = all_roots(meta, near, swap(near))
    last, roots = lax.optimization_barrier((arrived_parts[3], roots))
    return stats(meta, arrived_parts[:3] + [last]), roots


def solution(mesh):
    fine = Mesh(mesh.devices.reshape(4, 4, 2, 4), ("z", "y", "c", "x"))
    dp = ("z", "y", "c")
    return jax.shard_map(
        body,
        mesh=fine,
        in_specs=(P(dp, None, None, "x"), P(), P(dp, "x", None), P()),
        out_specs=(P(dp, "x", None), P(None, "x", None)),
        check_vma=False,
    )
```

```python
import jax
import jax.numpy as jnp
from jax import lax
from jax.experimental import pallas as pl
from jax.experimental.pallas import tpu as pltpu
from jax.sharding import Mesh, PartitionSpec as P

ITERS = 2
K = 256
Q = 64
T = 16
L = 128
STEP = 8
PART = 2
SWAP = K + 32
SENT = K + 16
SEND = SENT + Q
PIECE = K + 8
f32 = jnp.float32
bf16 = jnp.bfloat16
ANY = pl.BlockSpec(memory_space=pl.ANY)


def iotas(rows):
    row = lax.broadcasted_iota(jnp.int32, (rows, L), 0)
    lane = lax.broadcasted_iota(jnp.int32, (rows, L), 1)
    return row, lane


def pick_masks(m):
    row, lane = iotas(Q)
    odd = m % 2
    below = ((lane - Q * odd) < row).astype(jnp.int32)
    right = (lane >= Q).astype(jnp.int32)
    from_diag = jnp.maximum(right, below) * (1 - odd) + right * below * odd
    return from_diag > 0, lane == row + Q * odd


def pack(rows, m, masks):
    t0, t1 = rows[:, :L], rows[:, L:]
    if isinstance(m, int):
        diag_tile, other = (t0, t1) if m < 2 else (t1, t0)
    else:
        diag_tile = jnp.where(m < 2, t0, t1)
        other = jnp.where(m < 2, t1, t0)
    from_diag, on_diag = masks
    packed = jnp.where(from_diag, diag_tile, other)
    spread = jnp.where(on_diag, diag_tile, 0.0)
    diag = spread[:8]
    for i in range(8, Q, 8):
        diag = diag + spread[i:i + 8]
    return packed, diag


def split_diag(d):
    hi = d.astype(bf16).astype(f32)
    return (hi + pltpu.roll(d - hi, Q, 1)).astype(bf16)


def gram_of(g_refs, k):
    g = g_refs[k // PART][0, k % PART]
    return lax.dot_general(g, g, (((1,), (1,)), ((), ())), preferred_element_type=f32)


def gram_pack(gram, out_ref, k, masks, dtype):
    diags = []
    for m in range(4):
        packed, d = pack(gram[Q * m:Q * (m + 1)], m, masks[m])
        out_ref[k, Q * m:Q * (m + 1), :] = packed.astype(dtype)
        diags.append(d)
    return jnp.concatenate(diags, axis=0)


def gram_send_kernel(meta, *refs):
    g_refs, out_ref = refs[:-1], refs[-1]
    masks = [pick_masks(m) for m in range(4)]
    for k in range(STEP):
        out_ref[k, K:, :] = split_diag(gram_pack(gram_of(g_refs, k), out_ref, k, masks, bf16))


def rank_of(owner_ref, f, o):
    return lax.fori_loop(0, f, lambda g, n: n + (owner_ref[g] == o).astype(jnp.int32), jnp.int32(0))


def gram_keep_kernel(meta, *refs):
    g_refs, out_ref = refs[:-1], refs[-1]
    masks = [pick_masks(m) for m in range(4)]
    for k in range(STEP):
        out_ref[k, K:, :] = gram_pack(gram_of(g_refs, k), out_ref, k, masks, f32)


def merge_kernel(scale, meta, owner_ref, own_ref, got_ref, mine, theirs, out_ref, parts, diags):
    x, c, zy = meta[0], meta[1], meta[2]
    quarter = pl.ds(pl.multiple_of(Q * x, Q), Q)
    owners = [owner_ref[c * 16 + j] for j in range(16)]
    row, lane = iotas(32)
    odd = (row // 8) % 2
    own_half = (lane >= Q * odd) & (lane < Q * odd + Q)
    for j in range(16):
        out_ref[j, :K, :] = ((own_ref[j, :K, :] + got_ref[j, :K, :].astype(f32)) * scale).astype(bf16)
        got = got_ref[j, K:, :].astype(f32)
        got = jnp.where(own_half, got + pltpu.roll(got, Q, 1), 0.0)
        diags[j] = (own_ref[j, K:, :] + got) * scale
        parts[j] = (own_ref[j, quarter, :] + got_ref[j, quarter, :].astype(f32)) * scale
    for j in range(16):
        @pl.when(owners[j] // 2 == zy)
        def _(j=j):
            o = owners[j]
            r = rank_of(owner_ref, c * 16 + j, o)
            pick = jnp.where(o % 2 == c, 1.0, 0.0)
            old = mine[r] * pick + theirs[r] * (1.0 - pick)
            packed, d = pack(old, x, pick_masks(x))
            parts[j] += packed
            diags[j, pl.ds(pl.multiple_of(8 * x, 8), 8), :] += d

    last, _ = iotas(16)
    for j in range(16):
        high = parts[j].astype(bf16)
        out_ref[j, quarter, :] = high
        out_ref[j, SENT:, :] = (parts[j] - high.astype(f32)).astype(bf16)
        diag = jnp.zeros((16, L), f32)
        for m in range(4):
            diag = jnp.where(last == m, jnp.sum(diags[j, 8 * m:8 * m + 8, :], axis=0, keepdims=True), diag)
        out_ref[j, K:SENT, :] = split_diag(diag)


def params(mib):
    return pltpu.CompilerParams(vmem_limit_bytes=mib * 2**20)


GRAM_COST = pl.CostEstimate(flops=32 * K * K * 512, bytes_accessed=16 * K * 512 * 2 + 2**21, transcendentals=0)


def gram_call(kernel, core_of, dtype, name, meta, grads):
    parts = STEP // PART
    per = 16 // PART

    def part(p):
        return pl.BlockSpec((1, PART, K, 512), lambda i, meta: (0, core_of(meta[1]) * per + i * parts + p, 0, 0))

    return pl.pallas_call(
        kernel,
        grid_spec=pltpu.PrefetchScalarGridSpec(
            num_scalar_prefetch=1,
            grid=(16 // STEP,),
            in_specs=[part(p) for p in range(parts)],
            out_specs=pl.BlockSpec((STEP, SWAP, L), lambda i, meta: (i, 0, 0)),
        ),
        out_shape=jax.ShapeDtypeStruct((16, SWAP, L), dtype),
        compiler_params=params(48),
        cost_estimate=GRAM_COST,
        name=name,
    )(meta, *([grads] * parts))


def merge(scale, meta, owner, own, got, mine, theirs):
    whole = pl.BlockSpec((16, SWAP, L), lambda i, *_: (0, 0, 0))
    old = pl.BlockSpec((3, Q, K), lambda i, *_: (0, 0, 0))

    def kernel(*refs):
        merge_kernel(scale, *refs)

    return pl.pallas_call(
        kernel,
        grid_spec=pltpu.PrefetchScalarGridSpec(
            num_scalar_prefetch=2,
            grid=(1,),
            in_specs=[whole, whole, old, old],
            out_specs=pl.BlockSpec((16, SEND, L), lambda i, *_: (0, 0, 0)),
            scratch_shapes=[pltpu.VMEM((16, Q, L), f32), pltpu.VMEM((16, 32, L), f32)],
        ),
        out_shape=jax.ShapeDtypeStruct((16, SEND, L), bf16),
        compiler_params=params(24),
        cost_estimate=pl.CostEstimate(flops=2**20, bytes_accessed=2**22, transcendentals=0),
        name="merge",
    )(meta, owner, own, got, mine, theirs)


def plane_sum_kernel(arrived, out_ref):
    for m in range(4):
        rows = slice(Q * m, Q * (m + 1))
        total = arrived[0, rows, :].astype(f32)
        for j in range(1, 16):
            total = total + arrived[j, rows, :].astype(f32)
        for y in range(4):
            total = total + arrived[4 * m + y, SENT:, :].astype(f32)
        out_ref[rows, :] = total
    total = arrived[0, K:SENT, :].astype(f32)
    for j in range(1, 16):
        total = total + arrived[j, K:SENT, :].astype(f32)
    out_ref[K:, :] = total[:8]


def plane_sum(arrived):
    return pl.pallas_call(
        plane_sum_kernel,
        grid=(1,),
        in_specs=[pl.BlockSpec((16, SEND, L), lambda i: (0, 0, 0))],
        out_specs=pl.BlockSpec((PIECE, L), lambda i: (0, 0)),
        out_shape=jax.ShapeDtypeStruct((PIECE, L), f32),
        compiler_params=params(16),
        name="plane_sum",
    )(arrived)


def unpack(total, half):
    row, lane = iotas(Q)
    ends = total[K:]
    ends = ends + pltpu.roll(ends, Q, 1)
    for m in range(4):
        odd = m % 2
        part = total[Q * m:Q * (m + 1)]
        below = (lane - Q * odd) < row
        equal = lane == row + Q * odd
        right = lane >= Q
        from_diag = (right | below) if odd == 0 else (right & below)
        diag_tile = jnp.where(from_diag, part, 0.0)
        other = jnp.where(from_diag, 0.0, part)
        if m >= 2:
            other = jnp.where(equal, 0.0, other)
        diag_tile = diag_tile + jnp.where(equal, 0.5 * ends[m:m + 1], 0.0)
        tiles = (diag_tile, other) if m < 2 else (other, diag_tile)
        half[Q * m:Q * (m + 1), :L] = tiles[0]
        half[Q * m:Q * (m + 1), L:] = tiles[1]
    h = half[...]
    return h + h.T


def halves(a):
    high = a.astype(bf16)
    return high, (a - high.astype(f32)).astype(bf16)


def mm(a, b):
    (ah, al), (bh, bl) = halves(a), halves(b)
    dot = lambda u, v: jnp.dot(u, v, preferred_element_type=f32)
    return (dot(al, bh) + dot(ah, bl)) + dot(ah, bh)


def fourth_kernel(meta, root_ref, out_ref, copy_ref):
    r = root_ref[0]
    copy_ref[...] = r
    square = jnp.dot(r, r, preferred_element_type=f32)
    out_ref[...] = mm(square, square)


def fourth(meta, prev_roots):
    whole = pl.BlockSpec((K, K), lambda i, meta: (0, 0))
    return pl.pallas_call(
        fourth_kernel,
        grid_spec=pltpu.PrefetchScalarGridSpec(
            num_scalar_prefetch=1,
            grid=(1,),
            in_specs=[pl.BlockSpec((1, K, K), lambda i, meta: (meta[3], 0, 0))],
            out_specs=[whole, whole],
        ),
        out_shape=[jax.ShapeDtypeStruct((K, K), f32), jax.ShapeDtypeStruct((K, K), bf16)],
        compiler_params=params(8),
        cost_estimate=pl.CostEstimate(flops=14 * K**3, bytes_accessed=6 * K * K, transcendentals=0),
        name="fourth",
    )(meta, prev_roots)


def newton_kernel(meta, root_ref, fourth_ref, *refs):
    pieces, (out_ref, held, half) = refs[:4], refs[4:]
    z = meta[4]
    for s in range(4):
        held[lax.rem(z - s + 4, 4)] = pieces[s][...]
    factor = unpack(((held[0] + held[1]) + held[2]) + held[3], half)
    half[...] = factor
    row = lax.broadcasted_iota(jnp.int32, (K, K), 0)
    col = lax.broadcasted_iota(jnp.int32, (K, K), 1)
    five = jnp.where(row == col, 5.0, 0.0)
    coupled = mm(fourth_ref[...], factor)
    root = root_ref[...].astype(f32)
    for iteration in range(ITERS):
        update = (five - coupled) * 0.25
        root = mm(root, update)
        if iteration + 1 < ITERS:
            square = mm(update, update)
            coupled = mm(mm(square, square), coupled)
    root = root.astype(bf16)
    for j in range(16):
        rows = slice(Q * (j // 4), Q * (j // 4 + 1))
        out_ref[j, :Q] = root[rows]
        part = half[pl.ds(pl.multiple_of(Q * (j // 4) + T * z, T), T), :]
        high = part.astype(bf16)
        out_ref[j, Q:Q + T] = high
        out_ref[j, Q + T:] = (part - high.astype(f32)).astype(bf16)


def newton(meta, root, power, pieces):
    whole = pl.BlockSpec((K, K), lambda i, meta: (0, 0))
    piece = pl.BlockSpec((PIECE, L), lambda i, meta: (0, 0))
    return pl.pallas_call(
        newton_kernel,
        grid_spec=pltpu.PrefetchScalarGridSpec(
            num_scalar_prefetch=1,
            grid=(1,),
            in_specs=[whole, whole] + [piece] * 4,
            out_specs=pl.BlockSpec((16, Q + 2 * T, K), lambda i, meta: (0, 0, 0)),
            scratch_shapes=[pltpu.VMEM((4, PIECE, L), f32), pltpu.VMEM((K, K), f32)],
        ),
        out_shape=jax.ShapeDtypeStruct((16, Q + 2 * T, K), bf16),
        compiler_params=params(16),
        cost_estimate=pl.CostEstimate(flops=60 * K**3, bytes_accessed=2**21, transcendentals=0),
        name="newton",
    )(meta, root, power, *pieces)


ARRIVED = pl.BlockSpec((16, Q + 2 * T, K), lambda i, *_: (0, 0, 0))
OWNED = jax.ShapeDtypeStruct((4, 3, T, K), f32)
SLICE = jax.ShapeDtypeStruct((3, T, K), f32)


def pick_kernel(meta, owner_ref, mine, keep_ref, give_ref, near_ref):
    c, y = meta[1], lax.rem(meta[2], 4)
    near_ref[...] = mine[:, :Q, :]
    keep_ref[...] = jnp.zeros(keep_ref.shape, f32)
    give_ref[...] = jnp.zeros(give_ref.shape, f32)
    first = [owner_ref[g] for g in range(16)]
    own = [owner_ref[16 * c + g] for g in range(16)]
    for j in range(16):
        o = own[j]

        @pl.when(lax.rem(o // 2, 4) == y)
        def _(j=j, o=o):
            r = jnp.int32(0)
            for g in range(16):
                r = r + (first[g] == o).astype(jnp.int32)
            r = r * c
            for g in range(j):
                r = r + (own[g] == o).astype(jnp.int32)
            rows = mine[j, Q:Q + T, :].astype(f32) + mine[j, Q + T:, :].astype(f32)

            @pl.when(lax.rem(o, 2) == c)
            def _():
                keep_ref[o // 8, r] = rows

            @pl.when(lax.rem(o, 2) != c)
            def _():
                give_ref[o // 8, r] = rows


def pick(meta, owner, mine):
    block = pl.BlockSpec((4, 3, T, K), lambda i, *_: (0, 0, 0, 0))
    near = pl.BlockSpec((16, Q, K), lambda i, *_: (0, 0, 0))
    return pl.pallas_call(
        pick_kernel,
        grid_spec=pltpu.PrefetchScalarGridSpec(
            num_scalar_prefetch=2, grid=(1,), in_specs=[ARRIVED], out_specs=[block, block, near]
        ),
        out_shape=[OWNED, OWNED, jax.ShapeDtypeStruct((16, Q, K), bf16)],
        compiler_params=params(12),
        name="pick",
    )(meta, owner, mine)


def spread_kernel(meta, keep, got, *out):
    z = meta[4]
    for s in range(4):
        plane = lax.rem(z + s, 4)
        out[s][...] = keep[plane] + got[plane]


def spread(meta, keep, got):
    block = pl.BlockSpec((4, 3, T, K), lambda i, *_: (0, 0, 0, 0))
    piece = pl.BlockSpec((3, T, K), lambda i, *_: (0, 0, 0))
    return pl.pallas_call(
        spread_kernel,
        grid_spec=pltpu.PrefetchScalarGridSpec(
            num_scalar_prefetch=1, grid=(1,), in_specs=[block, block], out_specs=[piece] * 4
        ),
        out_shape=[SLICE] * 4,
        compiler_params=params(12),
        name="spread",
    )(meta, keep, got)


def stats_kernel(meta, *refs):
    pieces, out_ref = refs[:4], refs[4]
    for s in range(4):
        rows = pl.ds(pl.multiple_of(T * lax.rem(meta[4] - s + 4, 4), T), T)
        out_ref[:, rows, :] = pieces[s][...]


def stats(meta, pieces):
    piece = pl.BlockSpec((3, T, K), lambda i, *_: (0, 0, 0))
    return pl.pallas_call(
        stats_kernel,
        grid_spec=pltpu.PrefetchScalarGridSpec(
            num_scalar_prefetch=1,
            grid=(1,),
            in_specs=[piece] * 4,
            out_specs=pl.BlockSpec((3, Q, K), lambda i, *_: (0, 0, 0)),
        ),
        out_shape=jax.ShapeDtypeStruct((3, Q, K), f32),
        compiler_params=params(12),
        name="stats",
    )(meta, *pieces)


def all_roots_kernel(meta, near, far, out_ref, sems):
    c = meta[1]
    copies = []
    for i in range(4):
        part = pl.ds(4 * i, 4)
        copies.append(pltpu.make_async_copy(near.at[part], out_ref.at[pl.ds(16 * c + 4 * i, 4)], sems.at[i]))
        copies.append(pltpu.make_async_copy(far.at[part], out_ref.at[pl.ds(16 * (1 - c) + 4 * i, 4)], sems.at[4 + i]))
    for copy in copies:
        copy.start()
    for copy in copies:
        copy.wait()


def all_roots(meta, near, far):
    block = pl.BlockSpec((16, Q, K), lambda i, *_: (0, 0, 0))
    return pl.pallas_call(
        all_roots_kernel,
        grid_spec=pltpu.PrefetchScalarGridSpec(
            num_scalar_prefetch=1,
            grid=(1,),
            in_specs=[block, block],
            out_specs=ANY,
            scratch_shapes=[pltpu.SemaphoreType.DMA((8,))],
        ),
        out_shape=jax.ShapeDtypeStruct((32, Q, K), bf16),
        compiler_params=params(12),
        cost_estimate=pl.CostEstimate(flops=0, bytes_accessed=2**21, transcendentals=0),
        name="all_roots",
    )(meta, near, far)


def swap(a):
    return lax.ppermute(a, "c", [(0, 1), (1, 0)])


def turn(a, s):
    return lax.ppermute(a, "z", [(i, (i + s) % 4) for i in range(4)])


def body(grads, owner, stats_old, prev_roots):
    z, y, c, x = (lax.axis_index(a) for a in ("z", "y", "c", "x"))
    scale = 1.0 / (32 * 2048)
    meta = jnp.stack([x, c, z * 4 + y, c * 16 + x * 4 + y, z]).astype(jnp.int32)
    their_old = swap(stats_old)
    got = swap(gram_call(gram_send_kernel, lambda core: 1 - core, bf16, "gram_send", meta, grads))
    own = gram_call(gram_keep_kernel, lambda core: core, f32, "gram_keep", meta, grads)
    outgoing = merge(scale, meta, owner, own, got, stats_old, their_old)
    arrived = lax.all_to_all(outgoing, ("x", "y"), 0, 0, tiled=True)
    piece = plane_sum(arrived)
    power, root = fourth(meta, prev_roots)
    pieces = [piece] + [turn(piece, s) for s in (1, 2, 3)]
    mine = lax.all_to_all(newton(meta, root, power, pieces), ("x", "y"), 0, 0, tiled=True)
    keep, give, near = pick(meta, owner, mine)
    parts = spread(meta, keep, swap(give))
    arrived_parts = [parts[0]] + [turn(parts[s], s) for s in (1, 2, 3)]
    roots = all_roots(meta, near, swap(near))
    last, roots = lax.optimization_barrier((arrived_parts[3], roots))
    return stats(meta, arrived_parts[:3] + [last]), roots


def solution(mesh):
    fine = Mesh(mesh.devices.reshape(4, 4, 2, 4), ("z", "y", "c", "x"))
    dp = ("z", "y", "c")
    return jax.shard_map(
        body,
        mesh=fine,
        in_specs=(P(dp, None, None, "x"), P(), P(dp, "x", None), P()),
        out_specs=(P(dp, "x", None), P(None, "x", None)),
        check_vma=False,
    )
```
